128 devices in a mesh: ep: 32 (over y, x, core), head: 4 (over z).
Axes of the slice: x: 4, y: 4, z: 4, core: 2. Of those that a mesh axis runs over, the one named last changes fastest.
Arguments:
- queries: bfloat16 [256, 128, 576], P('ep', 'head'), may hold values from -60 to 60
- latent_cache: bfloat16 [256, 1024, 576], P('ep'), may hold values from -6 to 6
- lengths: int32 [256], P('ep'), may hold values from 2 to 1024, as said below
- value_up: bfloat16 [128, 512, 128], P('head'), may hold values from -1 to 1
- output_weight: bfloat16 [16384, 7168], P('head', 'ep'), may hold values from -0.046875 to 0.046875
- residual: bfloat16 [256, 7168], P(None, 'ep'), may hold values from -6 to 6
- norm_gain: float32 [7168], P('ep'), may hold values from 0.1 to 1.9
- expert_ids: int32 [256, 8], replicated, may hold values from 0 to 31, all different within a row; in each aligned block of 256 rows (0 to 255, 256 to 511, ...) at most 128 rows name the same one
- expert_weight: float32 [256, 8], replicated, may hold values from 0.2 to 1
- gate_weight: bfloat16 [32, 7168, 1024], P('ep', None, 'head'), may hold values from -0.0625 to 0.0625
- up_weight: bfloat16 [32, 7168, 1024], P('ep', None, 'head'), may hold values from -0.0625 to 0.0625
- down_weight: bfloat16 [32, 1024, 7168], P('ep', 'head'), may hold values from -0.25 to 0.25
Outputs:
- mixed: bfloat16 [256, 7168], P(None, 'ep')
The draws below stay inside these ranges and needn't reach their ends.
Inputs may be any that keep to these rules, and one draw needn't show every extreme that they name: Every sequence's cache holds valid rows at positions 0 to lengths - 1; some sequence has a full cache of 1024 positions. `expert_ids`: no expert is chosen by more than 128 tokens; some expert is chosen by exactly 128. The experts of one token differ.
All inputs are finite; a program needn't handle non-finite values.
Results may differ from the reference program's by a relative error of at most 0.013.
Values may be sent and summed in bfloat16 or wider, within the bound.
No kernel may reach another device: no remote copies, remote signals or barrier semaphores. Data moves between devices by JAX's collectives and lax.ppermute only.
A program may use at most 128 MiB of HBM per device.

```python
import math
import jax
import jax.numpy as jnp
import numpy as np
from jax import lax

D = 7168
HEADS = 128
LATENT = 512
VDIM = 128
FF = 1024
TOPK = 8
CTX = 1024
KDIM = 576
TOKENS = 256
EXPERTS = 32
CAP = 128


def first_keys(key):
    return jnp.clip(jax.random.normal(key, (TOKENS, KDIM), jnp.float32), -6.0, 6.0)


def draw_latent_cache(key, part):
    leading = first_keys(key)
    key = jax.random.fold_in(key, 11)
    rest = jnp.clip(jax.random.normal(key, (TOKENS, CTX, KDIM), jnp.float32), -6.0, 6.0)
    rest = rest.at[:, 0, :].set(leading)
    return rest.astype(jnp.bfloat16)


def draw_queries(key, part):
    key = jax.random.fold_in(key, 12)
    base = jnp.clip(jax.random.normal(key, (TOKENS, HEADS, KDIM), jnp.float32), -6.0, 6.0)
    return base.astype(jnp.bfloat16)


def draw_lengths(key, part):
    key = jax.random.fold_in(key, 13)
    counts = jax.random.randint(key, (TOKENS,), 2, CTX + 1, jnp.int32)
    picked = jax.random.randint(jax.random.fold_in(key, 1), (), 0, TOKENS, jnp.int32)
    return counts.at[picked].set(CTX)


def block_levels(key, extent, cuts, least, top_value):
    def one(dim, shards_of):
        steps = jax.random.uniform(jax.random.fold_in(jax.random.fold_in(key, 6), dim), (shards_of,), jnp.float32, least / len(cuts), top_value / len(cuts))
        return jnp.repeat(jnp.exp(steps), extent[dim] // shards_of).reshape((-1,) + (1,) * (len(extent) - dim - 1))

    loudness = one(*cuts[0])
    for cut in cuts[1:]:
        loudness = loudness * one(*cut)
    return loudness


def routed_block(key, own, number, rows, amount, top, limit, slope):
    sequence = jax.random.permutation(key, amount)
    crowded, common = shares(amount, rows * top, limit, slope, True), shares(amount, rows * top, limit, slope, False)
    places = jnp.arange(amount)

    def named(tallies, rotation):
        used = int((tallies > 0).sum())
        fixed = max(1, used // 4)
        shifted = fixed + (places - fixed + rotation * (used - fixed)) % max(1, amount - fixed)
        return jnp.zeros((amount,), jnp.int32).at[sequence[jnp.where(places < fixed, places, shifted)]].set(jnp.asarray(tallies, jnp.int32))

    tallies = jnp.where(number % 4 == 0, named(crowded, number // 4), named(common, number - number // 4 - 1))
    mixed = jax.random.permutation(jax.random.fold_in(own, 3), amount)
    giver, taker = mixed[0:amount // 2 * 2:2], mixed[1:amount // 2 * 2:2]
    margin = jnp.minimum(tallies[giver] - 1, limit - tallies[taker]) // 2
    margin = jnp.where((giver == sequence[0]) | (taker == sequence[0]) | (tallies[taker] == 0), 0, jnp.maximum(margin, 0))
    shifted = jax.random.randint(jax.random.fold_in(own, 4), (amount // 2,), 0, 1 << 20) % (margin + 1)
    tallies = tallies.at[giver].add(-shifted).at[taker].add(shifted)
    members = jnp.searchsorted(jnp.cumsum(tallies), jnp.arange(rows * top), side="right").astype(jnp.int32)
    listing = members.reshape(top, rows).T
    listing = listing[jax.random.permutation(jax.random.fold_in(own, 1), rows)]
    rotation = jax.random.randint(jax.random.fold_in(own, 2), (rows, 1), 0, top)
    return jnp.take_along_axis(listing, (jnp.arange(top)[None, :] + rotation) % top, axis=1)


def shares(number_of, total, reach, skew, full):
    loads = [(1 << 20) // math.isqrt(grade ** skew) + 1 for grade in range(1, number_of + 1)]
    largest = reach if full else min(reach, max(-(-total // number_of), total * loads[0] // sum(loads)))
    least = 1 if total - largest >= number_of - 1 else 0
    given, surplus = [largest] + [least] * (number_of - 1), total - largest - least * (number_of - 1)
    while surplus > 0:
        movable = [i for i in range(1, number_of) if given[i] < largest] or [i for i in range(1, number_of) if given[i] < reach]
        whole, budget = sum([loads[i] for i in movable]), surplus
        for i in movable:
            more = min(reach - given[i], max(1, budget * loads[i] // whole), surplus)
            given[i] = given[i] + more
            surplus = surplus - more
    return np.array(given)


def gaussian(key, shape, spread, limit, pieces=(), kind=jnp.bfloat16):
    result = spread * jax.random.normal(key, shape, jnp.float32)
    if pieces:
        result = result * block_levels(key, shape, pieces, -0.22, 0.18)
    return jnp.clip(result, -limit, limit).astype(kind)


def setup_inputs(seed: int = 0) -> dict:
    seeds = jax.random.split(jax.random.key(seed), 13)
    queries = draw_queries(jax.random.fold_in(seeds[12], 71), 0)
    latent_cache = draw_latent_cache(jax.random.fold_in(seeds[12], 71), 0)
    lengths = draw_lengths(jax.random.fold_in(seeds[12], 71), 0)
    value_up = gaussian(seeds[3], (HEADS, LATENT, VDIM), (LATENT // 16) ** -0.5, 1.0, ((0, 4),))
    output_weight = gaussian(seeds[4], (HEADS * VDIM, D), (HEADS * VDIM) ** -0.5, 0.046875, ((0, 4), (1, 32)))
    residual = gaussian(seeds[5], (TOKENS, D), 1.0, 6.0, ((1, 32),))
    norm_gain = jnp.clip(1.0 + 0.18 * jax.random.normal(seeds[6], (D,), jnp.float32), 0.1, 1.9)
    expert_ids_keys = jax.random.split(jax.random.fold_in(seeds[7], 1), TOKENS // TOKENS)
    expert_ids_turns = jax.random.permutation(jax.random.fold_in(seeds[7], 3), TOKENS // TOKENS)
    expert_ids = jax.vmap(lambda own, number: routed_block(jax.random.fold_in(seeds[7], 2), own, number, TOKENS, EXPERTS, TOPK, CAP, 2))(expert_ids_keys, expert_ids_turns).reshape((TOKENS, TOPK))
    expert_weight = jnp.clip(jax.random.uniform(seeds[8], (TOKENS, TOPK), jnp.float32, 0.2, 1.0), 0.2, 1.0)
    gate_weight = gaussian(seeds[9], (EXPERTS, D, FF), D ** -0.5, 0.0625, ((0, 32), (2, 4)))
    up_weight = gaussian(seeds[10], (EXPERTS, D, FF), D ** -0.5, 0.0625, ((0, 32), (2, 4)))
    down_weight = gaussian(seeds[11], (EXPERTS, FF, D), (FF // 2) ** -0.5, 0.25, ((0, 32), (1, 4)))
    return {"queries": queries, "latent_cache": latent_cache, "lengths": lengths, "value_up": value_up, "output_weight": output_weight, "residual": residual, "norm_gain": norm_gain, "expert_ids": expert_ids, "expert_weight": expert_weight, "gate_weight": gate_weight, "up_weight": up_weight, "down_weight": down_weight}


SCORE_SCALE = 192.0 ** (-0.5)
NORM_EPS = 1e-06

def routing_slots(expert_ids, experts, capacity):
    flat_ids = expert_ids.reshape(-1)
    onehot = (flat_ids[:, None] == jnp.arange(experts, dtype=jnp.int32)[None, :]).astype(jnp.int32)
    slot_rank = lax.optimization_barrier(jnp.sum((jnp.cumsum(onehot, axis=0) - 1) * onehot, axis=1)).astype(jnp.int32)
    destination = (flat_ids * capacity + slot_rank).astype(jnp.int32)
    owners = (jnp.arange(flat_ids.shape[0], dtype=jnp.int32) // expert_ids.shape[1]).astype(jnp.int32)
    slot_owner = jnp.zeros((experts * capacity,), jnp.int32).at[destination].set(owners)
    filled = jnp.zeros((experts * capacity,), jnp.bool_).at[destination].set(True)
    return (destination, slot_rank, slot_owner, filled)

def expert_apply(rows, gate_part, up_part, down_part):
    gate_out = jnp.dot(rows, gate_part, preferred_element_type=jnp.float32)
    up_out = jnp.dot(rows, up_part, preferred_element_type=jnp.float32)
    hidden_units = (jax.nn.silu(gate_out) * up_out).astype(jnp.bfloat16)
    return jnp.dot(hidden_units, down_part, preferred_element_type=jnp.float32).astype(jnp.bfloat16)

def reference(queries, latent_cache, lengths, value_up, output_weight, residual, norm_gain, expert_ids, expert_weight, gate_weight, up_weight, down_weight):
    positions = jnp.arange(CTX, dtype=jnp.int32)

    def attend(item):
        query_rows, cache_rows, length = item
        scores = jnp.dot(query_rows, cache_rows.T, preferred_element_type=jnp.float32) * SCORE_SCALE
        allowed = positions[None, :] < length
        scores = jnp.where(allowed, scores, jnp.float32(-1e+30))
        row_peaks = lax.optimization_barrier(jnp.max(scores, axis=1, keepdims=True))
        exponents = jnp.exp(scores - row_peaks)
        attn_weights = (exponents / lax.optimization_barrier(jnp.sum(exponents, axis=1, keepdims=True))).astype(jnp.bfloat16)
        return jnp.dot(attn_weights, cache_rows[:, :LATENT], preferred_element_type=jnp.float32).astype(jnp.bfloat16)
    contexts = lax.map(attend, (queries, latent_cache, lengths))
    values = jnp.einsum('thl,hlv->thv', contexts.astype(jnp.float32), value_up.astype(jnp.float32))
    values = values.astype(jnp.bfloat16).reshape(TOKENS, HEADS * VDIM)
    attention = jnp.dot(values, output_weight, preferred_element_type=jnp.float32)
    stream = residual.astype(jnp.float32) + attention
    squares = lax.optimization_barrier(jnp.sum(stream * stream, axis=1, keepdims=True))
    normed = (stream * lax.rsqrt(squares / D + NORM_EPS) * norm_gain[None, :]).astype(jnp.bfloat16)
    destination, slot_rank, slot_owner, filled = routing_slots(expert_ids, EXPERTS, CAP)
    rows = jnp.where(filled[:, None], normed[slot_owner], jnp.zeros((), jnp.bfloat16))
    rows = rows.reshape(EXPERTS, CAP, D)

    def one_expert(item):
        return expert_apply(*item)
    outputs = lax.map(one_expert, (rows, gate_weight, up_weight, down_weight)).reshape(EXPERTS * CAP, D)
    picked = outputs[destination].astype(jnp.float32).reshape(TOKENS, TOPK, D)
    combined = lax.optimization_barrier(jnp.sum(picked * expert_weight[:, :, None], axis=1))
    return (stream + combined).astype(jnp.bfloat16)
```

```python
import jax
import jax.numpy as jnp
from jax import lax
from jax.experimental import pallas as pl
from jax.experimental.pallas import tpu as pltpu
from jax.sharding import PartitionSpec as P

D = 7168
SCORE_SCALE = 192.0 ** (-0.5)
NORM_EPS = 1e-06

TOKENS = 256
EXPERTS = 32
SLOTS = 128
COLS = 224
ROWS = 240
GROUP = 4
TOPK = 8

BF16 = jnp.bfloat16
F32 = jnp.float32

NT = (((1,), (1,)), ((), ()))
NN = (((1,), (0,)), ((), ()))
TN = (((0,), (0,)), ((), ()))


def dot(a, b, dims):
    return lax.dot_general(a, b, dims, preferred_element_type=F32)


def slot_onehot(rank_row):
    slots = lax.broadcasted_iota(jnp.int32, (SLOTS, TOKENS), 0).astype(F32)
    return jnp.where(slots == rank_row, 1.0, 0.0).astype(BF16)


def route_kernel(me_ref, ids_ref, weight_ref, rank_ref, slot_weight_ref, token_weight):
    experts = lax.broadcasted_iota(jnp.int32, (EXPERTS, TOKENS), 0)
    member = jnp.zeros((EXPERTS, TOKENS), F32)
    weight = jnp.zeros((EXPERTS, TOKENS), F32)
    for k in range(TOPK):
        hit = experts == ids_ref[k : k + 1, :]
        member = jnp.where(hit, 1.0, member)
        weight = jnp.where(hit, weight_ref[k : k + 1, :], weight)
    before = lax.broadcasted_iota(jnp.int32, (TOKENS, TOKENS), 0)
    after = lax.broadcasted_iota(jnp.int32, (TOKENS, TOKENS), 1)
    earlier = jnp.where(before < after, 1.0, 0.0).astype(BF16)
    rank = dot(member.astype(BF16), earlier, NN)
    rank_ref[...] = jnp.where(member > 0.0, rank, -1.0)
    token_weight[...] = weight
    me = me_ref[0]
    slots = lax.broadcasted_iota(jnp.int32, (SLOTS, TOKENS), 0).astype(F32)
    mine = slots == rank_ref[pl.ds(me, 1), :]
    held = jnp.where(mine, token_weight[pl.ds(me, 1), :], 0.0)
    slot_weight_ref[...] = jnp.broadcast_to(
        jnp.sum(held, axis=1, keepdims=True), (SLOTS, 128)
    )


def route(me, ids_t, weight_t):
    vmem = pl.BlockSpec(memory_space=pltpu.VMEM)
    return pl.pallas_call(
        route_kernel,
        out_shape=(
            jax.ShapeDtypeStruct((EXPERTS, TOKENS), F32),
            jax.ShapeDtypeStruct((SLOTS, 128), F32),
        ),
        in_specs=[pl.BlockSpec(memory_space=pltpu.SMEM), vmem, vmem],
        out_specs=(vmem, vmem),
        scratch_shapes=[pltpu.VMEM((EXPERTS, TOKENS), F32)],
        name="route",
    )(me, ids_t, weight_t)


def project_kernel(me_ref, weight_ref, mine_ref, other_ref, out_ref):
    core = lax.rem(me_ref[0], 2)
    half = TOKENS // 2
    column = lax.broadcasted_iota(jnp.int32, (TOKENS, TOKENS), 0)
    token = lax.broadcasted_iota(jnp.int32, (TOKENS, TOKENS), 1)
    second = (column >= half).astype(jnp.int32)
    within = column - second * half
    parity = jnp.where(second == 1, 1 - core, core)
    owner = ((within >> 3) * 2 + parity) * 8 + (within & 7)
    order = jnp.where(owner == token, 1.0, 0.0).astype(BF16)
    weight = weight_ref[...]
    first = dot(weight, mine_ref[...], NT).astype(BF16)
    last = dot(weight, other_ref[...], NT).astype(BF16)
    placed = dot(first, order[:half], NN) + dot(last, order[half:], NN)
    out_ref[...] = placed.astype(BF16)


def project(me, weight_t, mine, other):
    vmem = pl.BlockSpec(memory_space=pltpu.VMEM)
    return pl.pallas_call(
        project_kernel,
        out_shape=jax.ShapeDtypeStruct((COLS, TOKENS), BF16),
        in_specs=[pl.BlockSpec(memory_space=pltpu.SMEM), vmem, vmem, vmem],
        out_specs=vmem,
        compiler_params=pltpu.CompilerParams(vmem_limit_bytes=32 * 2**20),
        name="project",
    )(me, weight_t, mine, other)


def dispatch_kernel(p0, p1, p2, p3, residual_ref, gain_ref, rank_ref, stream_ref, out_ref):
    attention = (p0[...].astype(F32) + p2[...].astype(F32)) + (
        p1[...].astype(F32) + p3[...].astype(F32)
    )
    stream = residual_ref[...].astype(F32) + attention
    stream_ref[...] = stream
    squares = jnp.sum(stream * stream, axis=0, keepdims=True)
    high = squares.astype(BF16).astype(F32)
    low = squares - high
    tail = lax.broadcasted_iota(jnp.int32, (ROWS - COLS, TOKENS), 0)
    tail = jnp.where(tail == 0, high, jnp.where(tail == 1, low, 0.0))
    scaled = (stream * gain_ref[...]).astype(BF16)
    rows = jnp.concatenate([scaled, tail.astype(BF16)], axis=0)
    for e in range(EXPERTS):
        chosen = slot_onehot(rank_ref[e : e + 1, :])
        out_ref[e] = dot(rows, chosen, NT).astype(BF16)


def dispatch(parts, residual_t, gain, rank):
    vmem = pl.BlockSpec(memory_space=pltpu.VMEM)
    return pl.pallas_call(
        dispatch_kernel,
        out_shape=(
            jax.ShapeDtypeStruct((COLS, TOKENS), F32),
            jax.ShapeDtypeStruct((EXPERTS, ROWS, SLOTS), BF16),
        ),
        in_specs=[vmem] * 7,
        out_specs=(vmem, vmem),
        compiler_params=pltpu.CompilerParams(vmem_limit_bytes=32 * 2**20),
        name="dispatch",
    )(*parts, residual_t, gain, rank)


def expert_kernel(
    tail_ref, slot_weight_ref, rows_ref, gate_ref, up_ref, down_ref, out_ref, gate_sum, up_sum, hidden
):
    step = pl.program_id(0)
    steps = EXPERTS // GROUP

    @pl.when(step == 0)
    def _():
        gate_sum[...] = jnp.zeros_like(gate_sum)
        up_sum[...] = jnp.zeros_like(up_sum)

    @pl.when(step < steps)
    def _():
        gate = gate_sum[...]
        up = up_sum[...]
        for j in range(GROUP):
            rows = rows_ref[j, :COLS, :]
            gate = gate + dot(rows, gate_ref[j * COLS : (j + 1) * COLS, :], TN)
            up = up + dot(rows, up_ref[j * COLS : (j + 1) * COLS, :], TN)
        gate_sum[...] = gate
        up_sum[...] = up

    @pl.when(step == steps - 1)
    def _():
        parts = jnp.sum(tail_ref[...].astype(F32), axis=0)
        squares = jnp.sum(parts, axis=0, keepdims=True)
        factor = lax.rsqrt(squares / D + NORM_EPS)
        row = lax.broadcasted_iota(jnp.int32, (SLOTS, SLOTS), 0)
        column = lax.broadcasted_iota(jnp.int32, (SLOTS, SLOTS), 1)
        factor = jnp.sum(jnp.where(row == column, factor, 0.0), axis=1, keepdims=True)
        gate = gate_sum[...] * factor
        up = up_sum[...] * factor
        value = gate / (1.0 + jnp.exp(-gate)) * up
        hidden[...] = (value * slot_weight_ref[:, :1]).astype(BF16)

    @pl.when(step >= steps)
    def _():
        result = dot(hidden[...], down_ref[...], NN)
        out_ref[...] = result.T.astype(BF16).reshape(GROUP, COLS, SLOTS)


def expert(tail, slot_weight, rows, gate_weight, up_weight, down_weight):
    steps = EXPERTS // GROUP
    width = gate_weight.shape[1]
    whole = lambda *shape: pl.BlockSpec(shape, lambda i: (0,) * len(shape))
    first = lambda i: jnp.minimum(i, steps - 1)
    second = lambda i: jnp.maximum(i - steps, 0)
    return pl.pallas_call(
        expert_kernel,
        grid=(2 * steps,),
        out_shape=jax.ShapeDtypeStruct((EXPERTS, COLS, SLOTS), BF16),
        in_specs=[
            whole(EXPERTS, ROWS - COLS, SLOTS),
            whole(SLOTS, 128),
            pl.BlockSpec((GROUP, ROWS, SLOTS), lambda i: (first(i), 0, 0)),
            pl.BlockSpec((GROUP * COLS, width), lambda i: (first(i), 0)),
            pl.BlockSpec((GROUP * COLS, width), lambda i: (first(i), 0)),
            pl.BlockSpec((width, GROUP * COLS), lambda i: (0, second(i))),
        ],
        out_specs=pl.BlockSpec((GROUP, COLS, SLOTS), lambda i: (second(i), 0, 0)),
        scratch_shapes=[
            pltpu.VMEM((SLOTS, width), F32),
            pltpu.VMEM((SLOTS, width), F32),
            pltpu.VMEM((SLOTS, width), BF16),
        ],
        compiler_params=pltpu.CompilerParams(vmem_limit_bytes=32 * 2**20),
        name="expert",
    )(tail, slot_weight, rows, gate_weight, up_weight, down_weight)


def combine_kernel(returned_ref, rank_ref, out_ref):
    total = jnp.zeros((COLS, TOKENS), F32)
    for e in range(EXPERTS):
        total = total + dot(returned_ref[e], slot_onehot(rank_ref[e : e + 1, :]), NN)
    out_ref[...] = total.astype(BF16)


def combine(returned, rank):
    vmem = pl.BlockSpec(memory_space=pltpu.VMEM)
    return pl.pallas_call(
        combine_kernel,
        out_shape=jax.ShapeDtypeStruct((COLS, TOKENS), BF16),
        in_specs=[vmem, vmem],
        out_specs=vmem,
        compiler_params=pltpu.CompilerParams(vmem_limit_bytes=32 * 2**20),
        name="combine",
    )(returned, rank)


def around_z(part):
    size = lax.axis_size("head")
    return [part] + [
        lax.ppermute(part, "head", [(z, (z + step) % size) for z in range(size)])
        for step in range(1, size)
    ]


def per_device(
    queries,
    latent_cache,
    lengths,
    value_up,
    output_weight,
    residual,
    norm_gain,
    expert_ids,
    expert_weight,
    gate_weight,
    up_weight,
    down_weight,
):
    local_seqs = queries.shape[0]
    me = lax.axis_index("ep").astype(jnp.int32).reshape(1)
    rank, slot_weight = route(me, expert_ids.T, expert_weight.T)

    positions = jnp.arange(latent_cache.shape[1], dtype=jnp.int32)
    scores = (
        jnp.einsum("shd,scd->shc", queries, latent_cache, preferred_element_type=jnp.float32)
        * SCORE_SCALE
    )
    allowed = (positions[None, :] < lengths[:, None])[:, None, :]
    scores = jnp.where(allowed, scores, jnp.float32(-1e30))
    row_peaks = jnp.max(scores, axis=2, keepdims=True)
    exponents = jnp.exp(scores - row_peaks)
    attn_weights = (exponents / jnp.sum(exponents, axis=2, keepdims=True)).astype(jnp.bfloat16)
    latent_width = value_up.shape[1]
    contexts = jnp.einsum(
        "shc,scl->shl",
        attn_weights,
        latent_cache[:, :, :latent_width],
        preferred_element_type=jnp.float32,
    ).astype(jnp.bfloat16)
    values = jnp.einsum("shl,hlv->shv", contexts, value_up, preferred_element_type=jnp.float32)
    values = values.astype(jnp.bfloat16).reshape(local_seqs, -1)

    chips = EXPERTS // 2
    same_core = [[2 * chip + core for chip in range(chips)] for core in range(2)]
    copies = jnp.broadcast_to(values[None], (chips,) + values.shape)
    mine = lax.all_to_all(
        copies, "ep", split_axis=0, concat_axis=0, tiled=True, axis_index_groups=same_core
    ).reshape(chips * local_seqs, -1)
    other = lax.ppermute(mine, "ep", [(i, i ^ 1) for i in range(EXPERTS)])
    partial = project(me, output_weight.T, mine, other)

    stream, outgoing = dispatch(around_z(partial), residual.T, norm_gain[:, None], rank)
    arrived = lax.all_to_all(outgoing, "ep", split_axis=0, concat_axis=0, tiled=True)
    results = expert(
        arrived[:, COLS:, :], slot_weight, arrived, gate_weight[0], up_weight[0], down_weight[0]
    )
    returned = lax.all_to_all(results, "ep", split_axis=0, concat_axis=0, tiled=True)
    c0, c1, c2, c3 = around_z(combine(returned, rank))
    combined = (c0.astype(F32) + c2.astype(F32)) + (c1.astype(F32) + c3.astype(F32))
    return (stream + combined).astype(BF16).T


def solution(mesh):
    placed = (
        P("ep", "head", None),
        P("ep", None, None),
        P("ep"),
        P("head", None, None),
        P("head", "ep"),
        P(None, "ep"),
        P("ep"),
        P(),
        P(),
        P("ep", None, "head"),
        P("ep", None, "head"),
        P("ep", "head", None),
    )
    return jax.shard_map(
        per_device, mesh=mesh, in_specs=placed, out_specs=P(None, "ep"), check_vma=False
    )
```

```python
import jax
import jax.numpy as jnp
from jax import lax
from jax.experimental import pallas as pl
from jax.experimental.pallas import tpu as pltpu
from jax.sharding import PartitionSpec as P

D = 7168
SCORE_SCALE = 192.0 ** (-0.5)
NORM_EPS = 1e-06

TOKENS = 256
EXPERTS = 32
SLOTS = 128
COLS = 224
ROWS = 240
GROUP = 4
TOPK = 8
SEQS = 2

BF16 = jnp.bfloat16
F32 = jnp.float32

NT = (((1,), (1,)), ((), ()))
NN = (((1,), (0,)), ((), ()))
TN = (((0,), (0,)), ((), ()))


def dot(a, b, dims):
    return lax.dot_general(a, b, dims, preferred_element_type=F32)


def attend_kernel(lengths_ref, queries_ref, cache_ref, up_hbm, out_ref, contexts, up_ref, up_sem):
    step = pl.program_id(0)
    heads, latent, width = up_ref.shape
    up_copy = pltpu.make_async_copy(up_hbm, up_ref, up_sem)

    @pl.when(step == 0)
    def _():
        up_copy.start()

    for b in range(SEQS):
        seq = step * SEQS + b
        scores = dot(queries_ref[b], cache_ref[b], NN) * SCORE_SCALE
        positions = lax.broadcasted_iota(jnp.int32, scores.shape, 1)
        scores = jnp.where(positions < lengths_ref[seq], scores, -1e30)
        exponents = jnp.exp(scores - jnp.max(scores, axis=1, keepdims=True))
        probs = (exponents / jnp.sum(exponents, axis=1, keepdims=True)).astype(BF16)
        contexts[seq] = dot(probs, cache_ref[b, :latent, :], NT)

    @pl.when(step == pl.num_programs(0) - 1)
    def _():
        up_copy.wait()
        for h in range(heads):
            rows = contexts[:, h, :].astype(BF16)
            out_ref[:, h * width : (h + 1) * width] = dot(rows, up_ref[h], NN).astype(BF16)


def attend(lengths, queries, cache_t, value_up):
    seqs, heads, kdim = queries.shape
    context = cache_t.shape[2]
    _, latent, width = value_up.shape
    return pl.pallas_call(
        attend_kernel,
        grid=(seqs // SEQS,),
        out_shape=jax.ShapeDtypeStruct((seqs, heads * width), BF16),
        in_specs=[
            pl.BlockSpec(memory_space=pltpu.SMEM),
            pl.BlockSpec((SEQS, heads, kdim), lambda i: (i, 0, 0)),
            pl.BlockSpec((SEQS, kdim, context), lambda i: (i, 0, 0)),
            pl.BlockSpec(memory_space=pl.ANY),
        ],
        out_specs=pl.BlockSpec((seqs, heads * width), lambda i: (0, 0)),
        scratch_shapes=[
            pltpu.VMEM((seqs, heads, latent), F32),
            pltpu.VMEM(value_up.shape, BF16),
            pltpu.SemaphoreType.DMA,
        ],
        compiler_params=pltpu.CompilerParams(vmem_limit_bytes=61 * 2**20),
        name="attend",
    )(lengths, queries, cache_t, value_up)


def slot_onehot(rank_row):
    slots = lax.broadcasted_iota(jnp.int32, (SLOTS, TOKENS), 0).astype(F32)
    return jnp.where(slots == rank_row, 1.0, 0.0).astype(BF16)


def route_kernel(me_ref, ids_ref, weight_ref, rank_ref, slot_weight_ref, token_weight):
    experts = lax.broadcasted_iota(jnp.int32, (EXPERTS, TOKENS), 0)
    member = jnp.zeros((EXPERTS, TOKENS), F32)
    weight = jnp.zeros((EXPERTS, TOKENS), F32)
    for k in range(TOPK):
        hit = experts == ids_ref[k : k + 1, :]
        member = jnp.where(hit, 1.0, member)
        weight = jnp.where(hit, weight_ref[k : k + 1, :], weight)
    before = lax.broadcasted_iota(jnp.int32, (TOKENS, TOKENS), 0)
    after = lax.broadcasted_iota(jnp.int32, (TOKENS, TOKENS), 1)
    earlier = jnp.where(before < after, 1.0, 0.0).astype(BF16)
    rank = dot(member.astype(BF16), earlier, NN)
    rank_ref[...] = jnp.where(member > 0.0, rank, -1.0)
    token_weight[...] = weight
    me = me_ref[0]
    slots = lax.broadcasted_iota(jnp.int32, (SLOTS, TOKENS), 0).astype(F32)
    mine = slots == rank_ref[pl.ds(me, 1), :]
    held = jnp.where(mine, token_weight[pl.ds(me, 1), :], 0.0)
    slot_weight_ref[...] = jnp.broadcast_to(
        jnp.sum(held, axis=1, keepdims=True), (SLOTS, 128)
    )


def route(me, ids_t, weight_t):
    vmem = pl.BlockSpec(memory_space=pltpu.VMEM)
    return pl.pallas_call(
        route_kernel,
        out_shape=(
            jax.ShapeDtypeStruct((EXPERTS, TOKENS), F32),
            jax.ShapeDtypeStruct((SLOTS, 128), F32),
        ),
        in_specs=[pl.BlockSpec(memory_space=pltpu.SMEM), vmem, vmem],
        out_specs=(vmem, vmem),
        scratch_shapes=[pltpu.VMEM((EXPERTS, TOKENS), F32)],
        name="route",
    )(me, ids_t, weight_t)


def half_kernel(weight_ref, values_ref, out_ref):
    out_ref[...] = dot(weight_ref[...], values_ref[...], NT).astype(BF16)


def project_half(weight_t, values):
    vmem = pl.BlockSpec(memory_space=pltpu.VMEM)
    return pl.pallas_call(
        half_kernel,
        out_shape=jax.ShapeDtypeStruct((COLS, values.shape[0]), BF16),
        in_specs=[vmem, vmem],
        out_specs=vmem,
        compiler_params=pltpu.CompilerParams(vmem_limit_bytes=16 * 2**20),
        name="project_half",
    )(weight_t, values)


def project_kernel(me_ref, weight_ref, first_ref, other_ref, out_ref):
    core = lax.rem(me_ref[0], 2)
    half = TOKENS // 2
    column = lax.broadcasted_iota(jnp.int32, (TOKENS, TOKENS), 0)
    token = lax.broadcasted_iota(jnp.int32, (TOKENS, TOKENS), 1)
    second = (column >= half).astype(jnp.int32)
    within = column - second * half
    parity = jnp.where(second == 1, 1 - core, core)
    owner = ((within >> 3) * 2 + parity) * 8 + (within & 7)
    order = jnp.where(owner == token, 1.0, 0.0).astype(BF16)
    last = dot(weight_ref[...], other_ref[...], NT).astype(BF16)
    placed = dot(first_ref[...], order[:half], NN) + dot(last, order[half:], NN)
    out_ref[...] = placed.astype(BF16)


def project(me, weight_t, first, other):
    vmem = pl.BlockSpec(memory_space=pltpu.VMEM)
    return pl.pallas_call(
        project_kernel,
        out_shape=jax.ShapeDtypeStruct((COLS, TOKENS), BF16),
        in_specs=[pl.BlockSpec(memory_space=pltpu.SMEM), vmem, vmem, vmem],
        out_specs=vmem,
        compiler_params=pltpu.CompilerParams(vmem_limit_bytes=16 * 2**20),
        name="project",
    )(me, weight_t, first, other)


def dispatch_kernel(p0, p1, p2, p3, residual_ref, gain_ref, rank_ref, stream_ref, out_ref):
    attention = (p0[...].astype(F32) + p2[...].astype(F32)) + (
        p1[...].astype(F32) + p3[...].astype(F32)
    )
    stream = residual_ref[...].astype(F32) + attention
    stream_ref[...] = stream
    squares = jnp.sum(stream * stream, axis=0, keepdims=True)
    high = squares.astype(BF16).astype(F32)
    low = squares - high
    tail = lax.broadcasted_iota(jnp.int32, (ROWS - COLS, TOKENS), 0)
    tail = jnp.where(tail == 0, high, jnp.where(tail == 1, low, 0.0))
    scaled = (stream * gain_ref[...]).astype(BF16)
    rows = jnp.concatenate([scaled, tail.astype(BF16)], axis=0)
    for e in range(EXPERTS):
        chosen = slot_onehot(rank_ref[e : e + 1, :])
        out_ref[e] = dot(rows, chosen, NT).astype(BF16)


def dispatch(parts, residual_t, gain, rank):
    vmem = pl.BlockSpec(memory_space=pltpu.VMEM)
    return pl.pallas_call(
        dispatch_kernel,
        out_shape=(
            jax.ShapeDtypeStruct((COLS, TOKENS), F32),
            jax.ShapeDtypeStruct((EXPERTS, ROWS, SLOTS), BF16),
        ),
        in_specs=[vmem] * 7,
        out_specs=(vmem, vmem),
        compiler_params=pltpu.CompilerParams(vmem_limit_bytes=16 * 2**20),
        cost_estimate=pl.CostEstimate(
            flops=30_000_000_000, bytes_accessed=2 * EXPERTS * ROWS * SLOTS, transcendentals=0
        ),
        name="dispatch",
    )(*parts, residual_t, gain, rank)


def expert_kernel(slot_weight_ref, rows_ref, gate_ref, up_ref, down_ref, out_ref):
    width = gate_ref.shape[1]
    gate = jnp.zeros((SLOTS, width), F32)
    up = jnp.zeros((SLOTS, width), F32)
    parts = jnp.zeros((ROWS - COLS, SLOTS), F32)
    for j in range(EXPERTS):
        rows = rows_ref[j, :COLS, :]
        parts = parts + rows_ref[j, COLS:, :].astype(F32)
        gate = gate + dot(rows, gate_ref[j * COLS : (j + 1) * COLS, :], TN)
        up = up + dot(rows, up_ref[j * COLS : (j + 1) * COLS, :], TN)
    squares = jnp.sum(parts, axis=0, keepdims=True)
    factor = lax.rsqrt(squares / D + NORM_EPS)
    row = lax.broadcasted_iota(jnp.int32, (SLOTS, SLOTS), 0)
    column = lax.broadcasted_iota(jnp.int32, (SLOTS, SLOTS), 1)
    factor = jnp.sum(jnp.where(row == column, factor, 0.0), axis=1, keepdims=True)
    gate = gate * factor
    up = up * factor
    value = gate / (1.0 + jnp.exp(-gate)) * up
    hidden = (value * slot_weight_ref[:, :1]).astype(BF16)
    for j in range(EXPERTS // GROUP):
        result = dot(hidden, down_ref[:, j * GROUP * COLS : (j + 1) * GROUP * COLS], NN)
        out_ref[j * GROUP : (j + 1) * GROUP] = result.T.astype(BF16).reshape(GROUP, COLS, SLOTS)


def expert(slot_weight, rows, gate_weight, up_weight, down_weight):
    vmem = pl.BlockSpec(memory_space=pltpu.VMEM)
    return pl.pallas_call(
        expert_kernel,
        out_shape=jax.ShapeDtypeStruct((EXPERTS, COLS, SLOTS), BF16),
        in_specs=[vmem] * 5,
        out_specs=vmem,
        compiler_params=pltpu.CompilerParams(vmem_limit_bytes=32 * 2**20),
        name="expert",
    )(slot_weight, rows, gate_weight, up_weight, down_weight)


def combine_kernel(returned_ref, rank_ref, out_ref):
    total = jnp.zeros((COLS, TOKENS), F32)
    for e in range(EXPERTS):
        total = total + dot(returned_ref[e], slot_onehot(rank_ref[e : e + 1, :]), NN)
    out_ref[...] = total.astype(BF16)


def combine(returned, rank):
    vmem = pl.BlockSpec(memory_space=pltpu.VMEM)
    return pl.pallas_call(
        combine_kernel,
        out_shape=jax.ShapeDtypeStruct((COLS, TOKENS), BF16),
        in_specs=[vmem, vmem],
        out_specs=vmem,
        compiler_params=pltpu.CompilerParams(vmem_limit_bytes=16 * 2**20),
        name="combine",
    )(returned, rank)


def around_z(part):
    size = lax.axis_size("head")
    return [part] + [
        lax.ppermute(part, "head", [(z, (z + step) % size) for z in range(size)])
        for step in range(1, size)
    ]


def per_device(
    queries,
    latent_cache,
    lengths,
    value_up,
    output_weight,
    residual,
    norm_gain,
    expert_ids,
    expert_weight,
    gate_weight,
    up_weight,
    down_weight,
):
    local_seqs = queries.shape[0]
    me = lax.axis_index("ep").astype(jnp.int32).reshape(1)
    values = attend(lengths, queries, latent_cache.swapaxes(1, 2), value_up)

    chips = EXPERTS // 2
    same_core = [[2 * chip + core for chip in range(chips)] for core in range(2)]
    copies = jnp.broadcast_to(values[None], (chips,) + values.shape)
    mine = lax.all_to_all(
        copies, "ep", split_axis=0, concat_axis=0, tiled=True, axis_index_groups=same_core
    ).reshape(chips * local_seqs, -1)
    other = lax.ppermute(mine, "ep", [(i, i ^ 1) for i in range(EXPERTS)])
    first = project_half(output_weight.T, mine)
    rank, slot_weight = route(me, expert_ids.T, expert_weight.T)
    first, rank, slot_weight = lax.optimization_barrier((first, rank, slot_weight))
    partial = project(me, output_weight.T, first, other)

    stream, outgoing = dispatch(around_z(partial), residual.T, norm_gain[:, None], rank)
    arrived = lax.all_to_all(outgoing, "ep", split_axis=0, concat_axis=0, tiled=True)
    results = expert(slot_weight, arrived, gate_weight[0], up_weight[0], down_weight[0])
    returned = lax.all_to_all(results, "ep", split_axis=0, concat_axis=0, tiled=True)
    c0, c1, c2, c3 = around_z(combine(returned, rank))
    combined = (c0.astype(F32) + c2.astype(F32)) + (c1.astype(F32) + c3.astype(F32))
    return (stream + combined).astype(BF16).T


def solution(mesh):
    placed = (
        P("ep", "head", None),
        P("ep", None, None),
        P("ep"),
        P("head", None, None),
        P("head", "ep"),
        P(None, "ep"),
        P("ep"),
        P(),
        P(),
        P("ep", None, "head"),
        P("ep", None, "head"),
        P("ep", "head", None),
    )
    return jax.shard_map(
        per_device, mesh=mesh, in_specs=placed, out_specs=P(None, "ep"), check_vma=False
    )
```

```python
import jax
import jax.numpy as jnp
from jax import lax
from jax.experimental import pallas as pl
from jax.experimental.pallas import tpu as pltpu
from jax.sharding import PartitionSpec as P

D = 7168
SCORE_SCALE = 192.0 ** (-0.5)
NORM_EPS = 1e-06

TOKENS = 256
EXPERTS = 32
SLOTS = 128
COLS = 224
ROWS = 240
GROUP = 4
TOPK = 8
PACKED = 16
SEQS = 4

BF16 = jnp.bfloat16
F32 = jnp.float32

NT = (((1,), (1,)), ((), ()))
NN = (((1,), (0,)), ((), ()))
TN = (((0,), (0,)), ((), ()))


def dot(a, b, dims):
    return lax.dot_general(a, b, dims, preferred_element_type=F32)


def attend_kernel(
    lengths_ref, queries_ref, cache_ref, up_hbm, out_ref, contexts, up_ref, scores, probs, up_sem
):
    step = pl.program_id(0)
    heads, latent, width = up_ref.shape
    context = cache_ref.shape[2]
    up_copy = pltpu.make_async_copy(up_hbm, up_ref, up_sem)

    @pl.when(step == 0)
    def _():
        up_copy.start()

    for b in range(SEQS):
        scores[b] = dot(queries_ref[b], cache_ref[b], NN)
    for b in range(SEQS):
        seq = step * SEQS + b
        positions = lax.broadcasted_iota(jnp.int32, (PACKED, context), 1)
        allowed = positions < lengths_ref[seq]
        for r in range(0, heads, PACKED):
            part = jnp.where(allowed, scores[b, r : r + PACKED] * SCORE_SCALE, -1e30)
            exponents = jnp.exp(part - jnp.max(part, axis=1, keepdims=True))
            total = jnp.sum(exponents, axis=1, keepdims=True)
            probs[b, r : r + PACKED] = (exponents / total).astype(BF16)
        contexts[seq] = dot(probs[b], cache_ref[b, :latent, :], NT)

    @pl.when(step == pl.num_programs(0) - 1)
    def _():
        up_copy.wait()
        for h in range(heads):
            rows = contexts[:, h, :].astype(BF16)
            values = dot(rows, up_ref[h], NN).astype(BF16)
            for copy in range(out_ref.shape[0]):
                out_ref[copy, :, h * width : (h + 1) * width] = values


def attend(lengths, queries, cache_t, value_up, copies):
    seqs, heads, kdim = queries.shape
    context = cache_t.shape[2]
    _, latent, width = value_up.shape
    return pl.pallas_call(
        attend_kernel,
        grid=(seqs // SEQS,),
        out_shape=jax.ShapeDtypeStruct((copies, seqs, heads * width), BF16),
        in_specs=[
            pl.BlockSpec(memory_space=pltpu.SMEM),
            pl.BlockSpec((SEQS, heads, kdim), lambda i: (i, 0, 0)),
            pl.BlockSpec((SEQS, kdim, context), lambda i: (i, 0, 0)),
            pl.BlockSpec(memory_space=pl.ANY),
        ],
        out_specs=pl.BlockSpec((copies, seqs, heads * width), lambda i: (0, 0, 0)),
        scratch_shapes=[
            pltpu.VMEM((seqs, heads, latent), F32),
            pltpu.VMEM(value_up.shape, BF16),
            pltpu.VMEM((SEQS, heads, context), F32),
            pltpu.VMEM((SEQS, heads, context), BF16),
            pltpu.SemaphoreType.DMA,
        ],
        compiler_params=pltpu.CompilerParams(vmem_limit_bytes=63 * 2**20),
        name="attend",
    )(lengths, queries, cache_t, value_up)


def slot_onehot(rank_row):
    slots = lax.broadcasted_iota(jnp.int32, (SLOTS, TOKENS), 0).astype(F32)
    return jnp.where(slots == rank_row, 1.0, 0.0).astype(BF16)


def route_kernel(
    me_ref, ids_ref, weight_ref, residual_ref, rank_ref, slot_weight_ref, residual_out, order_ref,
    token_rank, token_weight,
):
    experts = lax.broadcasted_iota(jnp.int32, (EXPERTS, TOKENS), 0)
    member = jnp.zeros((EXPERTS, TOKENS), F32)
    weight = jnp.zeros((EXPERTS, TOKENS), F32)
    for k in range(TOPK):
        hit = experts == ids_ref[k : k + 1, :]
        member = jnp.where(hit, 1.0, member)
        weight = jnp.where(hit, weight_ref[k : k + 1, :], weight)
    row = lax.broadcasted_iota(jnp.int32, (TOKENS, TOKENS), 0)
    column = lax.broadcasted_iota(jnp.int32, (TOKENS, TOKENS), 1)
    earlier = jnp.where(row < column, 1.0, 0.0).astype(BF16)
    rank = jnp.where(member > 0.0, dot(member.astype(BF16), earlier, NN), -1.0)
    token_rank[...] = rank
    token_weight[...] = weight
    me = me_ref[0]
    slots = lax.broadcasted_iota(jnp.int32, (SLOTS, TOKENS), 0).astype(F32)
    mine = slots == token_rank[pl.ds(me, 1), :]
    held = jnp.where(mine, token_weight[pl.ds(me, 1), :], 0.0)
    slot_weight_ref[...] = jnp.broadcast_to(
        jnp.sum(held, axis=1, keepdims=True), (SLOTS, 128)
    )
    core = lax.rem(me, 2)
    second = (column >= TOKENS // 2).astype(jnp.int32)
    within = column - second * (TOKENS // 2)
    parity = jnp.where(second == 1, 1 - core, core)
    token = ((within >> 3) * 2 + parity) * 8 + (within & 7)
    order = jnp.where(row == token, 1.0, 0.0).astype(BF16)
    order_ref[...] = order
    rank_ref[...] = dot(rank.astype(BF16), order, NN)
    residual_out[...] = dot(residual_ref[...], order, NN).astype(BF16)


def route(me, ids_t, weight_t, residual_t):
    vmem = pl.BlockSpec(memory_space=pltpu.VMEM)
    return pl.pallas_call(
        route_kernel,
        out_shape=(
            jax.ShapeDtypeStruct((EXPERTS, TOKENS), F32),
            jax.ShapeDtypeStruct((SLOTS, 128), F32),
            jax.ShapeDtypeStruct((COLS, TOKENS), BF16),
            jax.ShapeDtypeStruct((TOKENS, TOKENS), BF16),
        ),
        in_specs=[pl.BlockSpec(memory_space=pltpu.SMEM), vmem, vmem, vmem],
        out_specs=(vmem,) * 4,
        scratch_shapes=[pltpu.VMEM((EXPERTS, TOKENS), F32), pltpu.VMEM((EXPERTS, TOKENS), F32)],
        compiler_params=pltpu.CompilerParams(vmem_limit_bytes=8 * 2**20),
        name="route",
    )(me, ids_t, weight_t, residual_t)


def half_kernel(weight_ref, values_ref, out_ref):
    out_ref[...] = dot(weight_ref[...], values_ref[...], NT).astype(BF16)


def project_half(weight_t, values):
    vmem = pl.BlockSpec(memory_space=pltpu.VMEM)
    return pl.pallas_call(
        half_kernel,
        out_shape=jax.ShapeDtypeStruct((COLS, values.shape[0]), BF16),
        in_specs=[vmem, vmem],
        out_specs=vmem,
        compiler_params=pltpu.CompilerParams(vmem_limit_bytes=16 * 2**20),
        name="project_half",
    )(weight_t, values)


def project_kernel(weight_ref, first_ref, other_ref, out_ref):
    half = other_ref.shape[0]
    out_ref[:, :half] = first_ref[...]
    out_ref[:, half:] = dot(weight_ref[...], other_ref[...], NT).astype(BF16)


def project(weight_t, first, other):
    vmem = pl.BlockSpec(memory_space=pltpu.VMEM)
    return pl.pallas_call(
        project_kernel,
        out_shape=jax.ShapeDtypeStruct((COLS, TOKENS), BF16),
        in_specs=[vmem, vmem, vmem],
        out_specs=vmem,
        compiler_params=pltpu.CompilerParams(vmem_limit_bytes=16 * 2**20),
        name="project",
    )(weight_t, first, other)


def dispatch_kernel(p0, p1, p2, p3, residual_ref, gain_ref, rank_ref, stream_ref, out_ref):
    attention = (p0[...].astype(F32) + p2[...].astype(F32)) + (
        p1[...].astype(F32) + p3[...].astype(F32)
    )
    stream = residual_ref[...].astype(F32) + attention
    stream_ref[...] = stream
    squares = jnp.sum(stream * stream, axis=0, keepdims=True)
    high = squares.astype(BF16).astype(F32)
    low = squares - high
    tail = lax.broadcasted_iota(jnp.int32, (ROWS - COLS, TOKENS), 0)
    tail = jnp.where(tail == 0, high, jnp.where(tail == 1, low, 0.0))
    scaled = (stream * gain_ref[...]).astype(BF16)
    rows = jnp.concatenate([scaled, tail.astype(BF16)], axis=0)
    for e in range(EXPERTS):
        chosen = slot_onehot(rank_ref[e : e + 1, :])
        out_ref[e] = dot(rows, chosen, NT).astype(BF16)


def dispatch(parts, residual_t, gain, rank):
    vmem = pl.BlockSpec(memory_space=pltpu.VMEM)
    return pl.pallas_call(
        dispatch_kernel,
        out_shape=(
            jax.ShapeDtypeStruct((COLS, TOKENS), F32),
            jax.ShapeDtypeStruct((EXPERTS, ROWS, SLOTS), BF16),
        ),
        in_specs=[vmem] * 7,
        out_specs=(vmem, vmem),
        compiler_params=pltpu.CompilerParams(vmem_limit_bytes=16 * 2**20),
        cost_estimate=pl.CostEstimate(
            flops=30_000_000_000, bytes_accessed=2 * EXPERTS * ROWS * SLOTS, transcendentals=0
        ),
        name="dispatch",
    )(*parts, residual_t, gain, rank)


def expert_kernel(slot_weight_ref, rows_ref, gate_ref, up_ref, down_ref, out_ref):
    width = gate_ref.shape[1]
    gate = jnp.zeros((SLOTS, width), F32)
    up = jnp.zeros((SLOTS, width), F32)
    parts = jnp.zeros((ROWS - COLS, SLOTS), F32)
    for j in range(EXPERTS):
        rows = rows_ref[j, :COLS, :]
        parts = parts + rows_ref[j, COLS:, :].astype(F32)
        gate = gate + dot(rows, gate_ref[j * COLS : (j + 1) * COLS, :], TN)
        up = up + dot(rows, up_ref[j * COLS : (j + 1) * COLS, :], TN)
    squares = jnp.sum(parts, axis=0, keepdims=True)
    factor = lax.rsqrt(squares / D + NORM_EPS)
    row = lax.broadcasted_iota(jnp.int32, (SLOTS, SLOTS), 0)
    column = lax.broadcasted_iota(jnp.int32, (SLOTS, SLOTS), 1)
    factor = jnp.sum(jnp.where(row == column, factor, 0.0), axis=1, keepdims=True)
    gate = gate * factor
    up = up * factor
    value = gate / (1.0 + jnp.exp(-gate)) * up
    hidden = (value * slot_weight_ref[:, :1]).astype(BF16)
    for j in range(EXPERTS // GROUP):
        result = dot(hidden, down_ref[:, j * GROUP * COLS : (j + 1) * GROUP * COLS], NN)
        out_ref[j * GROUP : (j + 1) * GROUP] = result.T.astype(BF16).reshape(GROUP, COLS, SLOTS)


def expert(slot_weight, rows, gate_weight, up_weight, down_weight):
    vmem = pl.BlockSpec(memory_space=pltpu.VMEM)
    return pl.pallas_call(
        expert_kernel,
        out_shape=jax.ShapeDtypeStruct((EXPERTS, COLS, SLOTS), BF16),
        in_specs=[vmem] * 5,
        out_specs=vmem,
        compiler_params=pltpu.CompilerParams(vmem_limit_bytes=32 * 2**20),
        name="expert",
    )(slot_weight, rows, gate_weight, up_weight, down_weight)


def combine_kernel(returned_ref, rank_ref, out_ref):
    total = jnp.zeros((COLS, TOKENS), F32)
    for e in range(EXPERTS):
        total = total + dot(returned_ref[e], slot_onehot(rank_ref[e : e + 1, :]), NN)
    out_ref[...] = total.astype(BF16)


def combine(returned, rank):
    vmem = pl.BlockSpec(memory_space=pltpu.VMEM)
    return pl.pallas_call(
        combine_kernel,
        out_shape=jax.ShapeDtypeStruct((COLS, TOKENS), BF16),
        in_specs=[vmem, vmem],
        out_specs=vmem,
        compiler_params=pltpu.CompilerParams(vmem_limit_bytes=16 * 2**20),
        name="combine",
    )(returned, rank)


def finish_kernel(stream_ref, c0, c1, c2, c3, order_ref, out_ref):
    combined = (c0[...].astype(F32) + c2[...].astype(F32)) + (
        c1[...].astype(F32) + c3[...].astype(F32)
    )
    mixed = (stream_ref[...] + combined).astype(BF16)
    out_ref[...] = dot(mixed, order_ref[...], NT).astype(BF16)


def finish(stream, parts, order):
    vmem = pl.BlockSpec(memory_space=pltpu.VMEM)
    return pl.pallas_call(
        finish_kernel,
        out_shape=jax.ShapeDtypeStruct((COLS, TOKENS), BF16),
        in_specs=[vmem] * 6,
        out_specs=vmem,
        compiler_params=pltpu.CompilerParams(vmem_limit_bytes=16 * 2**20),
        name="finish",
    )(stream, *parts, order)


def around_z(part):
    size = lax.axis_size("head")
    return [part] + [
        lax.ppermute(part, "head", [(z, (z + step) % size) for z in range(size)])
        for step in range(1, size)
    ]


def per_device(
    queries,
    latent_cache,
    lengths,
    value_up,
    output_weight,
    residual,
    norm_gain,
    expert_ids,
    expert_weight,
    gate_weight,
    up_weight,
    down_weight,
):
    local_seqs = queries.shape[0]
    me = lax.axis_index("ep").astype(jnp.int32).reshape(1)
    chips = EXPERTS // 2
    same_core = [[2 * chip + core for chip in range(chips)] for core in range(2)]
    copies = attend(lengths, queries, latent_cache.swapaxes(1, 2), value_up, chips)
    weight_t = output_weight.T
    mine = lax.all_to_all(
        copies, "ep", split_axis=0, concat_axis=0, tiled=True, axis_index_groups=same_core
    ).reshape(chips * local_seqs, -1)
    other = lax.ppermute(mine, "ep", [(i, i ^ 1) for i in range(EXPERTS)])
    first = project_half(weight_t, mine)
    partial = project(weight_t, first, other)
    rank, slot_weight, residual_t, order = route(
        me, expert_ids.T, expert_weight.T, residual.T
    )

    stream, outgoing = dispatch(around_z(partial), residual_t, norm_gain[:, None], rank)
    arrived = lax.all_to_all(outgoing, "ep", split_axis=0, concat_axis=0, tiled=True)
    results = expert(slot_weight, arrived, gate_weight[0], up_weight[0], down_weight[0])
    returned = lax.all_to_all(results, "ep", split_axis=0, concat_axis=0, tiled=True)
    return finish(stream, around_z(combine(returned, rank)), order).T


def solution(mesh):
    placed = (
        P("ep", "head", None),
        P("ep", None, None),
        P("ep"),
        P("head", None, None),
        P("head", "ep"),
        P(None, "ep"),
        P("ep"),
        P(),
        P(),
        P("ep", None, "head"),
        P("ep", None, "head"),
        P("ep", "head", None),
    )
    return jax.shard_map(
        per_device, mesh=mesh, in_specs=placed, out_specs=P(None, "ep"), check_vma=False
    )
```

```python
import jax
import jax.numpy as jnp
from jax import lax
from jax.experimental import pallas as pl
from jax.experimental.pallas import tpu as pltpu
from jax.sharding import PartitionSpec as P

D = 7168
SCORE_SCALE = 192.0 ** (-0.5)
NORM_EPS = 1e-06

TOKENS = 256
EXPERTS = 32
SLOTS = 128
COLS = 224
ROWS = 232
GROUP = 4
TOPK = 8
PACKED = 16
SEQS = 4

BF16 = jnp.bfloat16
F32 = jnp.float32

NT = (((1,), (1,)), ((), ()))
NN = (((1,), (0,)), ((), ()))
TN = (((0,), (0,)), ((), ()))


def dot(a, b, dims):
    return lax.dot_general(a, b, dims, preferred_element_type=F32)


def attend_kernel(
    lengths_ref, queries_ref, cache_ref, up_hbm, out_ref, contexts, up_ref, scores, probs, up_sem
):
    step = pl.program_id(0)
    heads, latent, width = up_ref.shape
    context = cache_ref.shape[2]
    up_copy = pltpu.make_async_copy(up_hbm, up_ref, up_sem)

    @pl.when(step == 0)
    def _():
        up_copy.start()

    for b in range(SEQS):
        scores[b] = dot(queries_ref[b], cache_ref[b], NN)
    for b in range(SEQS):
        seq = step * SEQS + b
        positions = lax.broadcasted_iota(jnp.int32, (PACKED, context), 1)
        allowed = positions < lengths_ref[seq]
        for r in range(0, heads, PACKED):
            part = jnp.where(allowed, scores[b, r : r + PACKED] * SCORE_SCALE, -1e30)
            exponents = jnp.exp(part - jnp.max(part, axis=1, keepdims=True))
            total = jnp.sum(exponents, axis=1, keepdims=True)
            probs[b, r : r + PACKED] = (exponents / total).astype(BF16)
        contexts[seq] = dot(probs[b], cache_ref[b, :latent, :], NT)

    @pl.when(step == pl.num_programs(0) - 1)
    def _():
        up_copy.wait()
        for h in range(heads):
            rows = contexts[:, h, :].astype(BF16)
            values = dot(rows, up_ref[h], NN).astype(BF16)
            for copy in range(out_ref.shape[0]):
                out_ref[copy, :, h * width : (h + 1) * width] = values


def attend(lengths, queries, cache_t, value_up, copies):
    seqs, heads, kdim = queries.shape
    context = cache_t.shape[2]
    _, latent, width = value_up.shape
    return pl.pallas_call(
        attend_kernel,
        grid=(seqs // SEQS,),
        out_shape=jax.ShapeDtypeStruct((copies, seqs, heads * width), BF16),
        in_specs=[
            pl.BlockSpec(memory_space=pltpu.SMEM),
            pl.BlockSpec((SEQS, heads, kdim), lambda i: (i, 0, 0)),
            pl.BlockSpec((SEQS, kdim, context), lambda i: (i, 0, 0)),
            pl.BlockSpec(memory_space=pl.ANY),
        ],
        out_specs=pl.BlockSpec((copies, seqs, heads * width), lambda i: (0, 0, 0)),
        scratch_shapes=[
            pltpu.VMEM((seqs, heads, latent), F32),
            pltpu.VMEM(value_up.shape, BF16),
            pltpu.VMEM((SEQS, heads, context), F32),
            pltpu.VMEM((SEQS, heads, context), BF16),
            pltpu.SemaphoreType.DMA,
        ],
        compiler_params=pltpu.CompilerParams(vmem_limit_bytes=63 * 2**20),
        name="attend",
    )(lengths, queries, cache_t, value_up)


def slot_onehot(rank_ref, first, count):
    slots = lax.broadcasted_iota(jnp.int32, (SLOTS, TOKENS), 0).astype(F32)
    return jnp.concatenate(
        [
            jnp.where(slots == rank_ref[e : e + 1, :], 1.0, 0.0).astype(BF16)
            for e in range(first, first + count)
        ],
        axis=0,
    )


def route_kernel(
    me_ref, ids_ref, weight_ref, residual_ref, rank_ref, slot_weight_ref, residual_out, order_ref,
    token_rank, token_weight,
):
    experts = lax.broadcasted_iota(jnp.int32, (EXPERTS, TOKENS), 0)
    member = jnp.zeros((EXPERTS, TOKENS), F32)
    weight = jnp.zeros((EXPERTS, TOKENS), F32)
    for k in range(TOPK):
        hit = experts == ids_ref[k : k + 1, :]
        member = jnp.where(hit, 1.0, member)
        weight = jnp.where(hit, weight_ref[k : k + 1, :], weight)
    row = lax.broadcasted_iota(jnp.int32, (TOKENS, TOKENS), 0)
    column = lax.broadcasted_iota(jnp.int32, (TOKENS, TOKENS), 1)
    earlier = jnp.where(row < column, 1.0, 0.0).astype(BF16)
    rank = jnp.where(member > 0.0, dot(member.astype(BF16), earlier, NN), -1.0)
    token_rank[...] = rank
    token_weight[...] = weight
    me = me_ref[0]
    slots = lax.broadcasted_iota(jnp.int32, (SLOTS, TOKENS), 0).astype(F32)
    mine = slots == token_rank[pl.ds(me, 1), :]
    held = jnp.where(mine, token_weight[pl.ds(me, 1), :], 0.0)
    slot_weight_ref[...] = jnp.broadcast_to(
        jnp.sum(held, axis=1, keepdims=True), (SLOTS, 128)
    )
    core = lax.rem(me, 2)
    second = (column >= TOKENS // 2).astype(jnp.int32)
    within = column - second * (TOKENS // 2)
    parity = jnp.where(second == 1, 1 - core, core)
    token = ((within >> 3) * 2 + parity) * 8 + (within & 7)
    order = jnp.where(row == token, 1.0, 0.0).astype(BF16)
    order_ref[...] = order
    rank_ref[...] = dot(rank.astype(BF16), order, NN)
    residual_out[...] = dot(residual_ref[...], order, NN).astype(BF16)


def route(me, ids_t, weight_t, residual_t):
    vmem = pl.BlockSpec(memory_space=pltpu.VMEM)
    return pl.pallas_call(
        route_kernel,
        out_shape=(
            jax.ShapeDtypeStruct((EXPERTS, TOKENS), F32),
            jax.ShapeDtypeStruct((SLOTS, 128), F32),
            jax.ShapeDtypeStruct((COLS, TOKENS), BF16),
            jax.ShapeDtypeStruct((TOKENS, TOKENS), BF16),
        ),
        in_specs=[pl.BlockSpec(memory_space=pltpu.SMEM), vmem, vmem, vmem],
        out_specs=(vmem,) * 4,
        scratch_shapes=[pltpu.VMEM((EXPERTS, TOKENS), F32), pltpu.VMEM((EXPERTS, TOKENS), F32)],
        compiler_params=pltpu.CompilerParams(vmem_limit_bytes=8 * 2**20),
        name="route",
    )(me, ids_t, weight_t, residual_t)


def half_kernel(weight_ref, values_ref, out_ref):
    out_ref[...] = dot(weight_ref[...], values_ref[...], NT).astype(BF16)


def project_half(weight_t, values):
    vmem = pl.BlockSpec(memory_space=pltpu.VMEM)
    return pl.pallas_call(
        half_kernel,
        out_shape=jax.ShapeDtypeStruct((COLS, values.shape[0]), BF16),
        in_specs=[vmem, vmem],
        out_specs=vmem,
        compiler_params=pltpu.CompilerParams(vmem_limit_bytes=16 * 2**20),
        name="project_half",
    )(weight_t, values)


def project_kernel(weight_ref, first_ref, other_ref, out_ref):
    half = other_ref.shape[0]
    out_ref[:, :half] = first_ref[...]
    out_ref[:, half:] = dot(weight_ref[...], other_ref[...], NT).astype(BF16)


def project(weight_t, first, other):
    vmem = pl.BlockSpec(memory_space=pltpu.VMEM)
    return pl.pallas_call(
        project_kernel,
        out_shape=jax.ShapeDtypeStruct((COLS, TOKENS), BF16),
        in_specs=[vmem, vmem, vmem],
        out_specs=vmem,
        compiler_params=pltpu.CompilerParams(vmem_limit_bytes=16 * 2**20),
        name="project",
    )(weight_t, first, other)


def dispatch_kernel(p0, p1, p2, p3, residual_ref, gain_ref, rank_ref, stream_ref, out_ref):
    attention = (p0[...].astype(F32) + p2[...].astype(F32)) + (
        p1[...].astype(F32) + p3[...].astype(F32)
    )
    stream = residual_ref[...].astype(F32) + attention
    stream_ref[...] = stream
    squares = jnp.sum(stream * stream, axis=0, keepdims=True)
    high = squares.astype(BF16).astype(F32)
    low = squares - high
    tail = lax.broadcasted_iota(jnp.int32, (ROWS - COLS, TOKENS), 0)
    tail = jnp.where(tail == 0, high, jnp.where(tail == 1, low, 0.0))
    scaled = (stream * gain_ref[...]).astype(BF16)
    rows = jnp.concatenate([scaled, tail.astype(BF16)], axis=0)
    for e in range(0, EXPERTS, 2):
        picked = dot(rows, slot_onehot(rank_ref, e, 2), NT).astype(BF16)
        out_ref[e] = picked[:, :SLOTS]
        out_ref[e + 1] = picked[:, SLOTS:]


def dispatch(parts, residual_t, gain, rank):
    vmem = pl.BlockSpec(memory_space=pltpu.VMEM)
    return pl.pallas_call(
        dispatch_kernel,
        out_shape=(
            jax.ShapeDtypeStruct((COLS, TOKENS), F32),
            jax.ShapeDtypeStruct((EXPERTS, ROWS, SLOTS), BF16),
        ),
        in_specs=[vmem] * 7,
        out_specs=(vmem, vmem),
        compiler_params=pltpu.CompilerParams(vmem_limit_bytes=16 * 2**20),
        cost_estimate=pl.CostEstimate(
            flops=30_000_000_000, bytes_accessed=2 * EXPERTS * ROWS * SLOTS, transcendentals=0
        ),
        name="dispatch",
    )(*parts, residual_t, gain, rank)


def expert_kernel(slot_weight_ref, rows_ref, gate_ref, up_ref, down_ref, out_ref):
    width = gate_ref.shape[1]
    gate = jnp.zeros((SLOTS, width), F32)
    up = jnp.zeros((SLOTS, width), F32)
    parts = jnp.zeros((ROWS - COLS, SLOTS), F32)
    for j in range(EXPERTS):
        parts = parts + rows_ref[j, COLS:, :].astype(F32)
    for j in range(0, EXPERTS, GROUP):
        rows = rows_ref[j : j + GROUP, :COLS, :].reshape(GROUP * COLS, SLOTS)
        gate = gate + dot(rows, gate_ref[j * COLS : (j + GROUP) * COLS, :], TN)
        up = up + dot(rows, up_ref[j * COLS : (j + GROUP) * COLS, :], TN)
    squares = jnp.sum(parts, axis=0, keepdims=True)
    factor = lax.rsqrt(squares / D + NORM_EPS)
    row = lax.broadcasted_iota(jnp.int32, (SLOTS, SLOTS), 0)
    column = lax.broadcasted_iota(jnp.int32, (SLOTS, SLOTS), 1)
    factor = jnp.sum(jnp.where(row == column, factor, 0.0), axis=1, keepdims=True)
    gate = gate * factor
    up = up * factor
    value = gate / (1.0 + jnp.exp(-gate)) * up
    hidden = (value * slot_weight_ref[:, :1]).astype(BF16)
    for j in range(EXPERTS // GROUP):
        result = dot(hidden, down_ref[:, j * GROUP * COLS : (j + 1) * GROUP * COLS], NN)
        out_ref[j * GROUP : (j + 1) * GROUP] = result.T.astype(BF16).reshape(GROUP, COLS, SLOTS)


def expert(slot_weight, rows, gate_weight, up_weight, down_weight):
    vmem = pl.BlockSpec(memory_space=pltpu.VMEM)
    return pl.pallas_call(
        expert_kernel,
        out_shape=jax.ShapeDtypeStruct((EXPERTS, COLS, SLOTS), BF16),
        in_specs=[vmem] * 5,
        out_specs=vmem,
        compiler_params=pltpu.CompilerParams(vmem_limit_bytes=32 * 2**20),
        name="expert",
    )(slot_weight, rows, gate_weight, up_weight, down_weight)


def combine_kernel(returned_ref, rank_ref, out_ref):
    total = jnp.zeros((COLS, TOKENS), F32)
    for e in range(0, EXPERTS, GROUP):
        rows = jnp.concatenate([returned_ref[e + i] for i in range(GROUP)], axis=1)
        total = total + dot(rows, slot_onehot(rank_ref, e, GROUP), NN)
    out_ref[...] = total.astype(BF16)


def combine(returned, rank):
    vmem = pl.BlockSpec(memory_space=pltpu.VMEM)
    return pl.pallas_call(
        combine_kernel,
        out_shape=jax.ShapeDtypeStruct((COLS, TOKENS), BF16),
        in_specs=[vmem, vmem],
        out_specs=vmem,
        compiler_params=pltpu.CompilerParams(vmem_limit_bytes=16 * 2**20),
        name="combine",
    )(returned, rank)


def finish_kernel(stream_ref, c0, c1, c2, c3, order_ref, out_ref):
    combined = (c0[...].astype(F32) + c2[...].astype(F32)) + (
        c1[...].astype(F32) + c3[...].astype(F32)
    )
    mixed = (stream_ref[...] + combined).astype(BF16)
    out_ref[...] = dot(mixed, order_ref[...], NT).astype(BF16)


def finish(stream, parts, order):
    vmem = pl.BlockSpec(memory_space=pltpu.VMEM)
    return pl.pallas_call(
        finish_kernel,
        out_shape=jax.ShapeDtypeStruct((COLS, TOKENS), BF16),
        in_specs=[vmem] * 6,
        out_specs=vmem,
        compiler_params=pltpu.CompilerParams(vmem_limit_bytes=16 * 2**20),
        name="finish",
    )(stream, *parts, order)


def around_z(part):
    size = lax.axis_size("head")
    return [part] + [
        lax.ppermute(part, "head", [(z, (z + step) % size) for z in range(size)])
        for step in range(1, size)
    ]


def per_device(
    queries,
    latent_cache,
    lengths,
    value_up,
    output_weight,
    residual,
    norm_gain,
    expert_ids,
    expert_weight,
    gate_weight,
    up_weight,
    down_weight,
):
    local_seqs = queries.shape[0]
    me = lax.axis_index("ep").astype(jnp.int32).reshape(1)
    chips = EXPERTS // 2
    same_core = [[2 * chip + core for chip in range(chips)] for core in range(2)]
    copies = attend(lengths, queries, latent_cache.swapaxes(1, 2), value_up, chips)
    weight_t = output_weight.T
    mine = lax.all_to_all(
        copies, "ep", split_axis=0, concat_axis=0, tiled=True, axis_index_groups=same_core
    ).reshape(chips * local_seqs, -1)
    other = lax.ppermute(mine, "ep", [(i, i ^ 1) for i in range(EXPERTS)])
    first = project_half(weight_t, mine)
    partial = project(weight_t, first, other)
    rank, slot_weight, residual_t, order = route(
        me, expert_ids.T, expert_weight.T, residual.T
    )

    stream, outgoing = dispatch(around_z(partial), residual_t, norm_gain[:, None], rank)
    arrived = lax.all_to_all(outgoing, "ep", split_axis=0, concat_axis=0, tiled=True)
    results = expert(slot_weight, arrived, gate_weight[0], up_weight[0], down_weight[0])
    returned = lax.all_to_all(results, "ep", split_axis=0, concat_axis=0, tiled=True)
    return finish(stream, around_z(combine(returned, rank)), order).T


def solution(mesh):
    placed = (
        P("ep", "head", None),
        P("ep", None, None),
        P("ep"),
        P("head", None, None),
        P("head", "ep"),
        P(None, "ep"),
        P("ep"),
        P(),
        P(),
        P("ep", None, "head"),
        P("ep", None, "head"),
        P("ep", "head", None),
    )
    return jax.shard_map(
        per_device, mesh=mesh, in_specs=placed, out_specs=P(None, "ep"), check_vma=False
    )
```

```python
import jax
import jax.numpy as jnp
from jax import lax
from jax.experimental import pallas as pl
from jax.experimental.pallas import tpu as pltpu
from jax.sharding import PartitionSpec as P

D = 7168
SCORE_SCALE = 192.0 ** (-0.5)
NORM_EPS = 1e-06

TOKENS = 256
EXPERTS = 32
SLOTS = 128
COLS = 224
ROWS = 232
GROUP = 8
TOPK = 8
PACKED = 16
SEQS = 4

BF16 = jnp.bfloat16
F32 = jnp.float32

NT = (((1,), (1,)), ((), ()))
NN = (((1,), (0,)), ((), ()))
TN = (((0,), (0,)), ((), ()))


def dot(a, b, dims):
    return lax.dot_general(a, b, dims, preferred_element_type=F32)


def attend_kernel(
    lengths_ref, queries_ref, cache_ref, up_hbm, out_ref, contexts, up_ref, scores, probs, up_sem
):
    step = pl.program_id(0)
    heads, latent, width = up_ref.shape
    context = cache_ref.shape[2]
    up_copy = pltpu.make_async_copy(up_hbm, up_ref, up_sem)

    @pl.when(step == 0)
    def _():
        up_copy.start()

    for b in range(SEQS):
        scores[b] = dot(queries_ref[b], cache_ref[b], NN)
    for b in range(SEQS):
        seq = step * SEQS + b
        positions = lax.broadcasted_iota(jnp.int32, (PACKED, context), 1)
        allowed = positions < lengths_ref[seq]
        for r in range(0, heads, PACKED):
            part = jnp.where(allowed, scores[b, r : r + PACKED] * SCORE_SCALE, -1e30)
            exponents = jnp.exp(part - jnp.max(part, axis=1, keepdims=True))
            total = jnp.sum(exponents, axis=1, keepdims=True)
            probs[b, r : r + PACKED] = (exponents / total).astype(BF16)
        contexts[seq] = dot(probs[b], cache_ref[b, :latent, :], NT)

    @pl.when(step == pl.num_programs(0) - 1)
    def _():
        up_copy.wait()
        for h in range(0, heads, 2):
            rows = jnp.concatenate([contexts[:, h, :], contexts[:, h + 1, :]], axis=0).astype(BF16)
            both = dot(rows, jnp.concatenate([up_ref[h], up_ref[h + 1]], axis=1), NN)
            seqs = both.shape[0] // 2
            values = jnp.concatenate([both[:seqs, :width], both[seqs:, width:]], axis=1)
            values = jnp.concatenate([values, values], axis=0).astype(BF16)
            for pair in range(out_ref.shape[0]):
                out_ref[pair, :, h * width : (h + 2) * width] = values


def attend(lengths, queries, cache_t, value_up, copies):
    seqs, heads, kdim = queries.shape
    context = cache_t.shape[2]
    _, latent, width = value_up.shape
    return pl.pallas_call(
        attend_kernel,
        grid=(seqs // SEQS,),
        out_shape=jax.ShapeDtypeStruct((copies // 2, 2 * seqs, heads * width), BF16),
        in_specs=[
            pl.BlockSpec(memory_space=pltpu.SMEM),
            pl.BlockSpec((SEQS, heads, kdim), lambda i: (i, 0, 0)),
            pl.BlockSpec((SEQS, kdim, context), lambda i: (i, 0, 0)),
            pl.BlockSpec(memory_space=pl.ANY),
        ],
        out_specs=pl.BlockSpec((copies // 2, 2 * seqs, heads * width), lambda i: (0, 0, 0)),
        scratch_shapes=[
            pltpu.VMEM((seqs, heads, latent), F32),
            pltpu.VMEM(value_up.shape, BF16),
            pltpu.VMEM((SEQS, heads, context), F32),
            pltpu.VMEM((SEQS, heads, context), BF16),
            pltpu.SemaphoreType.DMA,
        ],
        compiler_params=pltpu.CompilerParams(vmem_limit_bytes=63 * 2**20),
        name="attend",
    )(lengths, queries, cache_t, value_up).reshape(copies, seqs, heads * width)


def slot_onehot(rank_ref, first, count):
    slots = lax.broadcasted_iota(jnp.int32, (SLOTS, TOKENS), 0).astype(F32)
    return jnp.concatenate(
        [
            jnp.where(slots == rank_ref[e : e + 1, :], 1.0, 0.0).astype(BF16)
            for e in range(first, first + count)
        ],
        axis=0,
    )


def route_kernel(
    me_ref, ids_ref, weight_ref, residual_ref, rank_ref, slot_weight_ref, residual_out, order_ref,
    token_rank, token_weight,
):
    experts = lax.broadcasted_iota(jnp.int32, (EXPERTS, TOKENS), 0)
    member = jnp.zeros((EXPERTS, TOKENS), F32)
    weight = jnp.zeros((EXPERTS, TOKENS), F32)
    for k in range(TOPK):
        hit = experts == ids_ref[k : k + 1, :]
        member = jnp.where(hit, 1.0, member)
        weight = jnp.where(hit, weight_ref[k : k + 1, :], weight)
    row = lax.broadcasted_iota(jnp.int32, (TOKENS, TOKENS), 0)
    column = lax.broadcasted_iota(jnp.int32, (TOKENS, TOKENS), 1)
    earlier = jnp.where(row < column, 1.0, 0.0).astype(BF16)
    rank = jnp.where(member > 0.0, dot(member.astype(BF16), earlier, NN), -1.0)
    token_rank[...] = rank
    token_weight[...] = weight
    me = me_ref[0]
    slots = lax.broadcasted_iota(jnp.int32, (SLOTS, TOKENS), 0).astype(F32)
    mine = slots == token_rank[pl.ds(me, 1), :]
    held = jnp.where(mine, token_weight[pl.ds(me, 1), :], 0.0)
    slot_weight_ref[...] = jnp.broadcast_to(
        jnp.sum(held, axis=1, keepdims=True), (SLOTS, 128)
    )
    core = lax.rem(me, 2)
    second = (column >= TOKENS // 2).astype(jnp.int32)
    within = column - second * (TOKENS // 2)
    parity = jnp.where(second == 1, 1 - core, core)
    token = ((within >> 3) * 2 + parity) * 8 + (within & 7)
    order = jnp.where(row == token, 1.0, 0.0).astype(BF16)
    order_ref[...] = order
    rank_ref[...] = dot(rank.astype(BF16), order, NN)
    residual_out[...] = dot(residual_ref[...], order, NN).astype(BF16)


def route(me, ids_t, weight_t, residual_t):
    vmem = pl.BlockSpec(memory_space=pltpu.VMEM)
    return pl.pallas_call(
        route_kernel,
        out_shape=(
            jax.ShapeDtypeStruct((EXPERTS, TOKENS), F32),
            jax.ShapeDtypeStruct((SLOTS, 128), F32),
            jax.ShapeDtypeStruct((COLS, TOKENS), BF16),
            jax.ShapeDtypeStruct((TOKENS, TOKENS), BF16),
        ),
        in_specs=[pl.BlockSpec(memory_space=pltpu.SMEM), vmem, vmem, vmem],
        out_specs=(vmem,) * 4,
        scratch_shapes=[pltpu.VMEM((EXPERTS, TOKENS), F32), pltpu.VMEM((EXPERTS, TOKENS), F32)],
        compiler_params=pltpu.CompilerParams(vmem_limit_bytes=8 * 2**20),
        name="route",
    )(me, ids_t, weight_t, residual_t)


def half_kernel(weight_ref, values_ref, out_ref):
    out_ref[...] = dot(weight_ref[...], values_ref[...], NT).astype(BF16)


def project_half(weight_t, values):
    vmem = pl.BlockSpec(memory_space=pltpu.VMEM)
    return pl.pallas_call(
        half_kernel,
        out_shape=jax.ShapeDtypeStruct((COLS, values.shape[0]), BF16),
        in_specs=[vmem, vmem],
        out_specs=vmem,
        compiler_params=pltpu.CompilerParams(vmem_limit_bytes=16 * 2**20),
        name="project_half",
    )(weight_t, values)


def project_kernel(weight_ref, first_ref, other_ref, out_ref):
    half = other_ref.shape[0]
    out_ref[:, :half] = first_ref[...]
    out_ref[:, half:] = dot(weight_ref[...], other_ref[...], NT).astype(BF16)


def project(weight_t, first, other):
    vmem = pl.BlockSpec(memory_space=pltpu.VMEM)
    return pl.pallas_call(
        project_kernel,
        out_shape=jax.ShapeDtypeStruct((COLS, TOKENS), BF16),
        in_specs=[vmem, vmem, vmem],
        out_specs=vmem,
        compiler_params=pltpu.CompilerParams(vmem_limit_bytes=16 * 2**20),
        name="project",
    )(weight_t, first, other)


def dispatch_kernel(p0, p1, p2, p3, residual_ref, gain_ref, rank_ref, stream_ref, out_ref):
    attention = (p0[...].astype(F32) + p2[...].astype(F32)) + (
        p1[...].astype(F32) + p3[...].astype(F32)
    )
    stream = residual_ref[...].astype(F32) + attention
    stream_ref[...] = stream
    squares = jnp.sum(stream * stream, axis=0, keepdims=True)
    high = squares.astype(BF16).astype(F32)
    low = squares - high
    tail = lax.broadcasted_iota(jnp.int32, (ROWS - COLS, TOKENS), 0)
    tail = jnp.where(tail == 0, high, jnp.where(tail == 1, low, 0.0))
    scaled = (stream * gain_ref[...]).astype(BF16)
    rows = jnp.concatenate([scaled, tail.astype(BF16)], axis=0)
    for e in range(0, EXPERTS, 2):
        picked = dot(rows, slot_onehot(rank_ref, e, 2), NT).astype(BF16)
        out_ref[e] = picked[:, :SLOTS]
        out_ref[e + 1] = picked[:, SLOTS:]


def dispatch(parts, residual_t, gain, rank):
    vmem = pl.BlockSpec(memory_space=pltpu.VMEM)
    return pl.pallas_call(
        dispatch_kernel,
        out_shape=(
            jax.ShapeDtypeStruct((COLS, TOKENS), F32),
            jax.ShapeDtypeStruct((EXPERTS, ROWS, SLOTS), BF16),
        ),
        in_specs=[vmem] * 7,
        out_specs=(vmem, vmem),
        compiler_params=pltpu.CompilerParams(vmem_limit_bytes=16 * 2**20),
        cost_estimate=pl.CostEstimate(
            flops=30_000_000_000, bytes_accessed=2 * EXPERTS * ROWS * SLOTS, transcendentals=0
        ),
        name="dispatch",
    )(*parts, residual_t, gain, rank)


def expert_kernel(slot_weight_ref, rows_ref, gate_ref, up_ref, down_ref, out_ref):
    width = gate_ref.shape[1]
    gate = jnp.zeros((SLOTS, width), F32)
    up = jnp.zeros((SLOTS, width), F32)
    parts = jnp.zeros((ROWS - COLS, SLOTS), F32)
    for j in range(EXPERTS):
        parts = parts + rows_ref[j, COLS:, :].astype(F32)
    for j in range(0, EXPERTS, GROUP):
        rows = rows_ref[j : j + GROUP, :COLS, :].reshape(GROUP * COLS, SLOTS)
        gate = gate + dot(rows, gate_ref[j * COLS : (j + GROUP) * COLS, :], TN)
        up = up + dot(rows, up_ref[j * COLS : (j + GROUP) * COLS, :], TN)
    squares = jnp.sum(parts, axis=0, keepdims=True)
    factor = lax.rsqrt(squares / D + NORM_EPS)
    row = lax.broadcasted_iota(jnp.int32, (SLOTS, SLOTS), 0)
    column = lax.broadcasted_iota(jnp.int32, (SLOTS, SLOTS), 1)
    factor = jnp.sum(jnp.where(row == column, factor, 0.0), axis=1, keepdims=True)
    gate = gate * factor
    up = up * factor
    value = gate / (1.0 + jnp.exp(-gate)) * up
    hidden = (value * slot_weight_ref[:, :1]).astype(BF16)
    for j in range(EXPERTS // GROUP):
        result = dot(hidden, down_ref[:, j * GROUP * COLS : (j + 1) * GROUP * COLS], NN)
        out_ref[j * GROUP : (j + 1) * GROUP] = result.T.astype(BF16).reshape(GROUP, COLS, SLOTS)


def expert(slot_weight, rows, gate_weight, up_weight, down_weight):
    vmem = pl.BlockSpec(memory_space=pltpu.VMEM)
    return pl.pallas_call(
        expert_kernel,
        out_shape=jax.ShapeDtypeStruct((EXPERTS, COLS, SLOTS), BF16),
        in_specs=[vmem] * 5,
        out_specs=vmem,
        compiler_params=pltpu.CompilerParams(vmem_limit_bytes=32 * 2**20),
        name="expert",
    )(slot_weight, rows, gate_weight, up_weight, down_weight)


def combine_kernel(returned_ref, rank_ref, out_ref):
    total = jnp.zeros((COLS, TOKENS), F32)
    for e in range(0, EXPERTS, GROUP):
        rows = jnp.concatenate([returned_ref[e + i] for i in range(GROUP)], axis=1)
        total = total + dot(rows, slot_onehot(rank_ref, e, GROUP), NN)
    out_ref[...] = total.astype(BF16)


def combine(returned, rank):
    vmem = pl.BlockSpec(memory_space=pltpu.VMEM)
    return pl.pallas_call(
        combine_kernel,
        out_shape=jax.ShapeDtypeStruct((COLS, TOKENS), BF16),
        in_specs=[vmem, vmem],
        out_specs=vmem,
        compiler_params=pltpu.CompilerParams(vmem_limit_bytes=16 * 2**20),
        name="combine",
    )(returned, rank)


def finish_kernel(stream_ref, c0, c1, c2, c3, order_ref, out_ref):
    combined = (c0[...].astype(F32) + c2[...].astype(F32)) + (
        c1[...].astype(F32) + c3[...].astype(F32)
    )
    mixed = (stream_ref[...] + combined).astype(BF16)
    out_ref[...] = dot(mixed, order_ref[...], NT).astype(BF16)


def finish(stream, parts, order):
    vmem = pl.BlockSpec(memory_space=pltpu.VMEM)
    return pl.pallas_call(
        finish_kernel,
        out_shape=jax.ShapeDtypeStruct((COLS, TOKENS), BF16),
        in_specs=[vmem] * 6,
        out_specs=vmem,
        compiler_params=pltpu.CompilerParams(vmem_limit_bytes=16 * 2**20),
        name="finish",
    )(stream, *parts, order)


def around_z(part):
    size = lax.axis_size("head")
    return [part] + [
        lax.ppermute(part, "head", [(z, (z + step) % size) for z in range(size)])
        for step in range(1, size)
    ]


def per_device(
    queries,
    latent_cache,
    lengths,
    value_up,
    output_weight,
    residual,
    norm_gain,
    expert_ids,
    expert_weight,
    gate_weight,
    up_weight,
    down_weight,
):
    local_seqs = queries.shape[0]
    me = lax.axis_index("ep").astype(jnp.int32).reshape(1)
    chips = EXPERTS // 2
    same_core = [[2 * chip + core for chip in range(chips)] for core in range(2)]
    copies = attend(lengths, queries, latent_cache.swapaxes(1, 2), value_up, chips)
    weight_t = output_weight.T
    mine = lax.all_to_all(
        copies, "ep", split_axis=0, concat_axis=0, tiled=True, axis_index_groups=same_core
    ).reshape(chips * local_seqs, -1)
    other = lax.ppermute(mine, "ep", [(i, i ^ 1) for i in range(EXPERTS)])
    first = project_half(weight_t, mine)
    partial = project(weight_t, first, other)
    rank, slot_weight, residual_t, order = route(
        me, expert_ids.T, expert_weight.T, residual.T
    )

    stream, outgoing = dispatch(around_z(partial), residual_t, norm_gain[:, None], rank)
    arrived = lax.all_to_all(outgoing, "ep", split_axis=0, concat_axis=0, tiled=True)
    results = expert(slot_weight, arrived, gate_weight[0], up_weight[0], down_weight[0])
    returned = lax.all_to_all(results, "ep", split_axis=0, concat_axis=0, tiled=True)
    return finish(stream, around_z(combine(returned, rank)), order).T


def solution(mesh):
    placed = (
        P("ep", "head", None),
        P("ep", None, None),
        P("ep"),
        P("head", None, None),
        P("head", "ep"),
        P(None, "ep"),
        P("ep"),
        P(),
        P(),
        P("ep", None, "head"),
        P("ep", None, "head"),
        P("ep", "head", None),
    )
    return jax.shard_map(
        per_device, mesh=mesh, in_specs=placed, out_specs=P(None, "ep"), check_vma=False
    )
```

```python
import jax
import jax.numpy as jnp
from jax import lax
from jax.experimental import pallas as pl
from jax.experimental.pallas import tpu as pltpu
from jax.sharding import PartitionSpec as P

D = 7168
SCORE_SCALE = 192.0 ** (-0.5)
NORM_EPS = 1e-06

TOKENS = 256
EXPERTS = 32
SLOTS = 128
COLS = 224
ROWS = 232
GROUP = 8
TOPK = 8
PACKED = 16
SEQS = 4

BF16 = jnp.bfloat16
F32 = jnp.float32

NT = (((1,), (1,)), ((), ()))
NN = (((1,), (0,)), ((), ()))
TN = (((0,), (0,)), ((), ()))


def dot(a, b, dims):
    return lax.dot_general(a, b, dims, preferred_element_type=F32)


def attend_kernel(
    lengths_ref, queries_ref, *refs
):
    caches, (up_hbm, out_ref, contexts, up_ref, scores, probs, up_sem) = refs[:SEQS], refs[SEQS:]
    step = pl.program_id(0)
    heads, latent, width = up_ref.shape
    context = caches[0].shape[2]
    up_copy = pltpu.make_async_copy(up_hbm, up_ref, up_sem)

    @pl.when(step == 0)
    def _():
        up_copy.start()

    for b in range(SEQS):
        scores[b] = dot(queries_ref[b], caches[b][0], NN)
    for b in range(SEQS):
        seq = step * SEQS + b
        positions = lax.broadcasted_iota(jnp.int32, (PACKED, context), 1)
        allowed = positions < lengths_ref[seq]
        for r in range(0, heads, PACKED):
            part = jnp.where(allowed, scores[b, r : r + PACKED] * SCORE_SCALE, -1e30)
            exponents = jnp.exp(part - jnp.max(part, axis=1, keepdims=True))
            total = jnp.sum(exponents, axis=1, keepdims=True)
            probs[b, r : r + PACKED] = (exponents / total).astype(BF16)
        contexts[seq] = dot(probs[b], caches[b][0, :latent, :], NT)

    @pl.when(step == pl.num_programs(0) - 1)
    def _():
        up_copy.wait()
        for h in range(0, heads, 2):
            rows = jnp.concatenate([contexts[:, h, :], contexts[:, h + 1, :]], axis=0).astype(BF16)
            both = dot(rows, jnp.concatenate([up_ref[h], up_ref[h + 1]], axis=1), NN)
            seqs = both.shape[0] // 2
            values = jnp.concatenate([both[:seqs, :width], both[seqs:, width:]], axis=1)
            values = jnp.concatenate([values, values], axis=0).astype(BF16)
            for pair in range(out_ref.shape[0]):
                out_ref[pair, :, h * width : (h + 2) * width] = values


def attend(lengths, queries, cache_t, value_up, copies):
    seqs, heads, kdim = queries.shape
    context = cache_t.shape[2]
    _, latent, width = value_up.shape
    return pl.pallas_call(
        attend_kernel,
        grid=(seqs // SEQS,),
        out_shape=jax.ShapeDtypeStruct((copies // 2, 2 * seqs, heads * width), BF16),
        in_specs=[
            pl.BlockSpec(memory_space=pltpu.SMEM),
            pl.BlockSpec((SEQS, heads, kdim), lambda i: (i, 0, 0)),
            *(
                pl.BlockSpec((1, kdim, context), lambda i, b=b: (i * SEQS + b, 0, 0))
                for b in range(SEQS)
            ),
            pl.BlockSpec(memory_space=pl.ANY),
        ],
        out_specs=pl.BlockSpec((copies // 2, 2 * seqs, heads * width), lambda i: (0, 0, 0)),
        scratch_shapes=[
            pltpu.VMEM((seqs, heads, latent), F32),
            pltpu.VMEM(value_up.shape, BF16),
            pltpu.VMEM((SEQS, heads, context), F32),
            pltpu.VMEM((SEQS, heads, context), BF16),
            pltpu.SemaphoreType.DMA,
        ],
        compiler_params=pltpu.CompilerParams(vmem_limit_bytes=61 * 2**20),
        name="attend",
    )(lengths, queries, *[cache_t] * SEQS, value_up).reshape(copies, seqs, heads * width)


def slot_onehot(rank_ref, first, count):
    slots = lax.broadcasted_iota(jnp.int32, (SLOTS, TOKENS), 0).astype(F32)
    return jnp.concatenate(
        [
            jnp.where(slots == rank_ref[e : e + 1, :], 1.0, 0.0).astype(BF16)
            for e in range(first, first + count)
        ],
        axis=0,
    )


def route_kernel(
    me_ref, ids_ref, weight_ref, residual_ref, rank_ref, slot_weight_ref, residual_out, order_ref,
    token_rank, token_weight,
):
    experts = lax.broadcasted_iota(jnp.int32, (EXPERTS, TOKENS), 0)
    member = jnp.zeros((EXPERTS, TOKENS), F32)
    weight = jnp.zeros((EXPERTS, TOKENS), F32)
    for k in range(TOPK):
        hit = experts == ids_ref[k : k + 1, :]
        member = jnp.where(hit, 1.0, member)
        weight = jnp.where(hit, weight_ref[k : k + 1, :], weight)
    row = lax.broadcasted_iota(jnp.int32, (TOKENS, TOKENS), 0)
    column = lax.broadcasted_iota(jnp.int32, (TOKENS, TOKENS), 1)
    earlier = jnp.where(row < column, 1.0, 0.0).astype(BF16)
    rank = jnp.where(member > 0.0, dot(member.astype(BF16), earlier, NN), -1.0)
    token_rank[...] = rank
    token_weight[...] = weight
    me = me_ref[0]
    slots = lax.broadcasted_iota(jnp.int32, (SLOTS, TOKENS), 0).astype(F32)
    mine = slots == token_rank[pl.ds(me, 1), :]
    held = jnp.where(mine, token_weight[pl.ds(me, 1), :], 0.0)
    slot_weight_ref[...] = jnp.broadcast_to(
        jnp.sum(held, axis=1, keepdims=True), (SLOTS, 128)
    )
    core = lax.rem(me, 2)
    second = (column >= TOKENS // 2).astype(jnp.int32)
    within = column - second * (TOKENS // 2)
    parity = jnp.where(second == 1, 1 - core, core)
    token = ((within >> 3) * 2 + parity) * 8 + (within & 7)
    order = jnp.where(row == token, 1.0, 0.0).astype(BF16)
    order_ref[...] = order
    rank_ref[...] = dot(rank.astype(BF16), order, NN)
    residual_out[...] = dot(residual_ref[...], order, NN).astype(BF16)


def route(me, ids_t, weight_t, residual_t):
    vmem = pl.BlockSpec(memory_space=pltpu.VMEM)
    return pl.pallas_call(
        route_kernel,
        out_shape=(
            jax.ShapeDtypeStruct((EXPERTS, TOKENS), F32),
            jax.ShapeDtypeStruct((SLOTS, 128), F32),
            jax.ShapeDtypeStruct((COLS, TOKENS), BF16),
            jax.ShapeDtypeStruct((TOKENS, TOKENS), BF16),
        ),
        in_specs=[pl.BlockSpec(memory_space=pltpu.SMEM), vmem, vmem, vmem],
        out_specs=(vmem,) * 4,
        scratch_shapes=[pltpu.VMEM((EXPERTS, TOKENS), F32), pltpu.VMEM((EXPERTS, TOKENS), F32)],
        compiler_params=pltpu.CompilerParams(vmem_limit_bytes=8 * 2**20),
        name="route",
    )(me, ids_t, weight_t, residual_t)


def half_kernel(weight_ref, values_ref, out_ref):
    out_ref[...] = dot(weight_ref[...], values_ref[...], NT).astype(BF16)


def project_half(weight_t, values):
    vmem = pl.BlockSpec(memory_space=pltpu.VMEM)
    return pl.pallas_call(
        half_kernel,
        out_shape=jax.ShapeDtypeStruct((COLS, values.shape[0]), BF16),
        in_specs=[vmem, vmem],
        out_specs=vmem,
        compiler_params=pltpu.CompilerParams(vmem_limit_bytes=16 * 2**20),
        name="project_half",
    )(weight_t, values)


def project_kernel(weight_ref, first_ref, other_ref, out_ref):
    half = other_ref.shape[0]
    out_ref[:, :half] = first_ref[...]
    out_ref[:, half:] = dot(weight_ref[...], other_ref[...], NT).astype(BF16)


def project(weight_t, first, other):
    vmem = pl.BlockSpec(memory_space=pltpu.VMEM)
    return pl.pallas_call(
        project_kernel,
        out_shape=jax.ShapeDtypeStruct((COLS, TOKENS), BF16),
        in_specs=[vmem, vmem, vmem],
        out_specs=vmem,
        compiler_params=pltpu.CompilerParams(vmem_limit_bytes=16 * 2**20),
        name="project",
    )(weight_t, first, other)


def dispatch_kernel(p0, p1, p2, p3, residual_ref, gain_ref, rank_ref, stream_ref, out_ref):
    attention = (p0[...].astype(F32) + p2[...].astype(F32)) + (
        p1[...].astype(F32) + p3[...].astype(F32)
    )
    stream = residual_ref[...].astype(F32) + attention
    stream_ref[...] = stream
    squares = jnp.sum(stream * stream, axis=0, keepdims=True)
    high = squares.astype(BF16).astype(F32)
    low = squares - high
    tail = lax.broadcasted_iota(jnp.int32, (ROWS - COLS, TOKENS), 0)
    tail = jnp.where(tail == 0, high, jnp.where(tail == 1, low, 0.0))
    scaled = (stream * gain_ref[...]).astype(BF16)
    rows = jnp.concatenate([scaled, tail.astype(BF16)], axis=0)
    for e in range(0, EXPERTS, 2):
        picked = dot(rows, slot_onehot(rank_ref, e, 2), NT).astype(BF16)
        out_ref[e] = picked[:, :SLOTS]
        out_ref[e + 1] = picked[:, SLOTS:]


def dispatch(parts, residual_t, gain, rank):
    vmem = pl.BlockSpec(memory_space=pltpu.VMEM)
    return pl.pallas_call(
        dispatch_kernel,
        out_shape=(
            jax.ShapeDtypeStruct((COLS, TOKENS), F32),
            jax.ShapeDtypeStruct((EXPERTS, ROWS, SLOTS), BF16),
        ),
        in_specs=[vmem] * 7,
        out_specs=(vmem, vmem),
        compiler_params=pltpu.CompilerParams(vmem_limit_bytes=16 * 2**20),
        cost_estimate=pl.CostEstimate(
            flops=30_000_000_000, bytes_accessed=2 * EXPERTS * ROWS * SLOTS, transcendentals=0
        ),
        name="dispatch",
    )(*parts, residual_t, gain, rank)


def expert_kernel(slot_weight_ref, rows_ref, gate_ref, up_ref, down_ref, out_ref):
    width = gate_ref.shape[1]
    gate = jnp.zeros((SLOTS, width), F32)
    up = jnp.zeros((SLOTS, width), F32)
    parts = jnp.zeros((ROWS - COLS, SLOTS), F32)
    for j in range(EXPERTS):
        parts = parts + rows_ref[j, COLS:, :].astype(F32)
    for j in range(0, EXPERTS, GROUP):
        rows = rows_ref[j : j + GROUP, :COLS, :].reshape(GROUP * COLS, SLOTS)
        gate = gate + dot(rows, gate_ref[j * COLS : (j + GROUP) * COLS, :], TN)
        up = up + dot(rows, up_ref[j * COLS : (j + GROUP) * COLS, :], TN)
    squares = jnp.sum(parts, axis=0, keepdims=True)
    factor = lax.rsqrt(squares / D + NORM_EPS)
    row = lax.broadcasted_iota(jnp.int32, (SLOTS, SLOTS), 0)
    column = lax.broadcasted_iota(jnp.int32, (SLOTS, SLOTS), 1)
    factor = jnp.sum(jnp.where(row == column, factor, 0.0), axis=1, keepdims=True)
    gate = gate * factor
    up = up * factor
    value = gate / (1.0 + jnp.exp(-gate)) * up
    hidden = (value * slot_weight_ref[:, :1]).astype(BF16)
    for j in range(EXPERTS // GROUP):
        result = dot(hidden, down_ref[:, j * GROUP * COLS : (j + 1) * GROUP * COLS], NN)
        out_ref[j * GROUP : (j + 1) * GROUP] = result.T.astype(BF16).reshape(GROUP, COLS, SLOTS)


def expert(slot_weight, rows, gate_weight, up_weight, down_weight):
    vmem = pl.BlockSpec(memory_space=pltpu.VMEM)
    return pl.pallas_call(
        expert_kernel,
        out_shape=jax.ShapeDtypeStruct((EXPERTS, COLS, SLOTS), BF16),
        in_specs=[vmem] * 5,
        out_specs=vmem,
        compiler_params=pltpu.CompilerParams(vmem_limit_bytes=32 * 2**20),
        name="expert",
    )(slot_weight, rows, gate_weight, up_weight, down_weight)


def combine_kernel(returned_ref, rank_ref, out_ref):
    total = jnp.zeros((COLS, TOKENS), F32)
    for e in range(0, EXPERTS, GROUP):
        rows = jnp.concatenate([returned_ref[e + i] for i in range(GROUP)], axis=1)
        total = total + dot(rows, slot_onehot(rank_ref, e, GROUP), NN)
    out_ref[...] = total.astype(BF16)


def combine(returned, rank):
    vmem = pl.BlockSpec(memory_space=pltpu.VMEM)
    return pl.pallas_call(
        combine_kernel,
        out_shape=jax.ShapeDtypeStruct((COLS, TOKENS), BF16),
        in_specs=[vmem, vmem],
        out_specs=vmem,
        compiler_params=pltpu.CompilerParams(vmem_limit_bytes=16 * 2**20),
        name="combine",
    )(returned, rank)


def finish_kernel(stream_ref, c0, c1, c2, c3, order_ref, out_ref):
    combined = (c0[...].astype(F32) + c2[...].astype(F32)) + (
        c1[...].astype(F32) + c3[...].astype(F32)
    )
    mixed = (stream_ref[...] + combined).astype(BF16)
    out_ref[...] = dot(mixed, order_ref[...], NT).astype(BF16)


def finish(stream, parts, order):
    vmem = pl.BlockSpec(memory_space=pltpu.VMEM)
    return pl.pallas_call(
        finish_kernel,
        out_shape=jax.ShapeDtypeStruct((COLS, TOKENS), BF16),
        in_specs=[vmem] * 6,
        out_specs=vmem,
        compiler_params=pltpu.CompilerParams(vmem_limit_bytes=16 * 2**20),
        name="finish",
    )(stream, *parts, order)


def around_z(part):
    size = lax.axis_size("head")
    return [part] + [
        lax.ppermute(part, "head", [(z, (z + step) % size) for z in range(size)])
        for step in range(1, size)
    ]


def per_device(
    queries,
    latent_cache,
    lengths,
    value_up,
    output_weight,
    residual,
    norm_gain,
    expert_ids,
    expert_weight,
    gate_weight,
    up_weight,
    down_weight,
):
    local_seqs = queries.shape[0]
    me = lax.axis_index("ep").astype(jnp.int32).reshape(1)
    chips = EXPERTS // 2
    same_core = [[2 * chip + core for chip in range(chips)] for core in range(2)]
    copies = attend(lengths, queries, latent_cache.swapaxes(1, 2), value_up, chips)
    weight_t = output_weight.T
    mine = lax.all_to_all(
        copies, "ep", split_axis=0, concat_axis=0, tiled=True, axis_index_groups=same_core
    ).reshape(chips * local_seqs, -1)
    other = lax.ppermute(mine, "ep", [(i, i ^ 1) for i in range(EXPERTS)])
    first = project_half(weight_t, mine)
    partial = project(weight_t, first, other)
    rank, slot_weight, residual_t, order = route(
        me, expert_ids.T, expert_weight.T, residual.T
    )

    stream, outgoing = dispatch(around_z(partial), residual_t, norm_gain[:, None], rank)
    arrived = lax.all_to_all(outgoing, "ep", split_axis=0, concat_axis=0, tiled=True)
    results = expert(slot_weight, arrived, gate_weight[0], up_weight[0], down_weight[0])
    returned = lax.all_to_all(results, "ep", split_axis=0, concat_axis=0, tiled=True)
    return finish(stream, around_z(combine(returned, rank)), order).T


def solution(mesh):
    placed = (
        P("ep", "head", None),
        P("ep", None, None),
        P("ep"),
        P("head", None, None),
        P("head", "ep"),
        P(None, "ep"),
        P("ep"),
        P(),
        P(),
        P("ep", None, "head"),
        P("ep", None, "head"),
        P("ep", "head", None),
    )
    return jax.shard_map(
        per_device, mesh=mesh, in_specs=placed, out_specs=P(None, "ep"), check_vma=False
    )
```
